256 devices in a mesh: gx: 32 (over x_lo, z, core), gy: 8 (over y, x_hi).
Axes of the slice: x: 4 (x_hi: 2, x_lo: 2; x = x_hi * 2 + x_lo), y: 4, z: 8, core: 2. Of those that a mesh axis runs over, the one named last changes fastest.
Arguments:
- body_force: float32 [3, 512, 128, 256], P(None, 'gx', 'gy'), may hold values from -6 to 6
- phase: int32 [512, 128, 256], P('gx', 'gy'), may hold values from 0 to 7
- viscosity_table: float32 [8], replicated, may hold values from 0.001 to 1000
- wall_kinds: int32 [3, 6], replicated, may hold values from 0 to 1
Outputs:
- weighted_velocity: float32 [3, 512, 128, 256], P(None, 'gx', 'gy')
- residual: float32 [3, 512, 128, 256], P(None, 'gx', 'gy')
The draws below stay inside these ranges and needn't reach their ends.
Inputs may be any that keep to these rules, and one draw needn't show every extreme that they name: phase values are valid indices 0 to 7 into viscosity_table.
All inputs are finite; a program needn't handle non-finite values.
Results may differ from the reference program's by a relative error of at most 0.0003.
Values sent between devices are 32-bit elements; how exact they have to be, the bound alone decides.
A program may use at most 320 MiB of HBM per device.

```python
import math
import jax
import jax.numpy as jnp

NZ = 256
LEVELS = 4
SWEEPS = 2
CSWEEPS = 24
NPHASE = 8
NX = 512
NY = 128


def set_ends(values, stream_key, least, top_value):
    spot = [jax.random.randint(jax.random.fold_in(stream_key, axis), (), 0, length) for axis, length in enumerate(values.shape)]
    main_axis = values.shape.index(max(values.shape))
    next_to = spot[:main_axis] + [(spot[main_axis] + 1) % values.shape[main_axis]] + spot[main_axis + 1:]
    return values.at[tuple(spot)].set(least).at[tuple(next_to)].set(top_value)


def block_levels(own_key, shape, cuts, low, largest):
    def one(position, shards_of):
        draws = jax.random.uniform(jax.random.fold_in(jax.random.fold_in(own_key, 6), position), (shards_of,), jnp.float32, low / len(cuts), largest / len(cuts))
        return jnp.repeat(jnp.exp(draws), shape[position] // shards_of).reshape((-1,) + (1,) * (len(shape) - position - 1))

    gain = one(*cuts[0])
    for cut in cuts[1:]:
        gain = gain * one(*cut)
    return gain


def centred(stream_key, dims, scale, bound, cuts=(), kind=jnp.bfloat16):
    array = scale * jax.random.normal(stream_key, dims, jnp.float32)
    if cuts:
        array = array * block_levels(stream_key, dims, cuts, -0.22, 0.18)
    return jnp.clip(array, -bound, bound).astype(kind)


def setup_inputs(seed: int = 0) -> dict:
    splits = jax.random.split(jax.random.key(seed), 5)
    body_force = centred(splits[0], (3, NX, NY, NZ), 1.0, 6.0, ((1, 32), (2, 8)), jnp.float32)
    phase = set_ends(jax.random.randint(splits[1], (NX, NY, NZ), 0, NPHASE), jax.random.fold_in(splits[1], 1), 0, NPHASE - 1).astype(jnp.int32)
    viscosity_table = jnp.clip(jnp.exp(jax.random.uniform(splits[2], (NPHASE,), jnp.float32, math.log(0.001), math.log(1000.0))), 0.001, 1000.0)
    wall_kinds = set_ends(jax.random.randint(splits[3], (3, 6), 0, 2), jax.random.fold_in(splits[3], 1), 0, 1).astype(jnp.int32)
    return dict(body_force=body_force, phase=phase, viscosity_table=viscosity_table, wall_kinds=wall_kinds)


fine_low = 0.2
fine_high = 2.0
coarse_low = 0.05
coarse_high = 2.0


def wall_terms(viscosity, x_places, y_places, z_count, x_total, y_total, wall_kinds, scale):
    kinds = wall_kinds.astype(jnp.float32)
    z_places = jnp.arange(z_count, dtype=jnp.int32)
    x_low = (x_places == 0).astype(jnp.float32)[:, None, None]
    x_high = (x_places == x_total - 1).astype(jnp.float32)[:, None, None]
    y_low = (y_places == 0).astype(jnp.float32)[None, :, None]
    y_high = (y_places == y_total - 1).astype(jnp.float32)[None, :, None]
    z_low = (z_places == 0).astype(jnp.float32)[None, None, :]
    z_high = (z_places == z_count - 1).astype(jnp.float32)[None, None, :]
    total = kinds[:, 0, None, None, None] * x_low[None]
    total = total + kinds[:, 1, None, None, None] * x_high[None]
    total = total + kinds[:, 2, None, None, None] * y_low[None]
    total = total + kinds[:, 3, None, None, None] * y_high[None]
    total = total + kinds[:, 4, None, None, None] * z_low[None]
    total = total + kinds[:, 5, None, None, None] * z_high[None]
    return 2.0 * scale * viscosity[None] * total


def halve(values):
    lead = values.shape[:-3]
    x_count, y_count, z_count = values.shape[-3:]
    split = values.reshape(lead + (x_count // 2, 2, y_count // 2, 2, z_count // 2, 2))
    return jnp.mean(split, axis=(-5, -3, -1))


def widen(values):
    comps, x_count, y_count, z_count = values.shape
    spread = jnp.broadcast_to(values.reshape(comps, x_count, 1, y_count, 1, z_count, 1), (comps, x_count, 2, y_count, 2, z_count, 2))
    return spread.reshape(comps, 2 * x_count, 2 * y_count, 2 * z_count)


def build_whole(viscosity, wall_kinds, scale):
    x_count, y_count, z_count = viscosity.shape
    face_x = 0.5 * (viscosity[:-1] + viscosity[1:]) * scale
    face_y = 0.5 * (viscosity[:, :-1] + viscosity[:, 1:]) * scale
    face_z = 0.5 * (viscosity[:, :, :-1] + viscosity[:, :, 1:]) * scale
    zero_x = jnp.zeros((1, y_count, z_count), jnp.float32)
    zero_y = jnp.zeros((x_count, 1, z_count), jnp.float32)
    zero_z = jnp.zeros((x_count, y_count, 1), jnp.float32)
    sum_x = jnp.concatenate([zero_x, face_x], 0) + jnp.concatenate([face_x, zero_x], 0)
    sum_y = jnp.concatenate([zero_y, face_y], 1) + jnp.concatenate([face_y, zero_y], 1)
    sum_z = jnp.concatenate([zero_z, face_z], 2) + jnp.concatenate([face_z, zero_z], 2)
    walls = wall_terms(viscosity, jnp.arange(x_count, dtype=jnp.int32), jnp.arange(y_count, dtype=jnp.int32), z_count, x_count, y_count, wall_kinds, scale)
    diagonal = (sum_x + sum_y + sum_z)[None] + walls
    return face_x, face_y, face_z, diagonal


def apply_whole(field, level):
    face_x, face_y, face_z, diagonal = level
    comps, x_count, y_count, z_count = field.shape
    zero_x = jnp.zeros((1, y_count, z_count), jnp.float32)
    zero_y = jnp.zeros((x_count, 1, z_count), jnp.float32)
    zero_z = jnp.zeros((x_count, y_count, 1), jnp.float32)
    padded = jnp.pad(field, ((0, 0), (1, 1), (1, 1), (1, 1)))
    near = jnp.concatenate([zero_x, face_x], 0) * padded[:, :-2, 1:-1, 1:-1] + jnp.concatenate([face_x, zero_x], 0) * padded[:, 2:, 1:-1, 1:-1]
    near = near + jnp.concatenate([zero_y, face_y], 1) * padded[:, 1:-1, :-2, 1:-1] + jnp.concatenate([face_y, zero_y], 1) * padded[:, 1:-1, 2:, 1:-1]
    near = near + jnp.concatenate([zero_z, face_z], 2) * padded[:, 1:-1, 1:-1, :-2] + jnp.concatenate([face_z, zero_z], 2) * padded[:, 1:-1, 1:-1, 2:]
    return diagonal * field - near


def smooth_whole(resid, level, low, high, sweeps):
    middle = (high + low) / 2.0
    radius = (high - low) / 2.0
    relative = middle / radius
    ratio_now = 1.0 / relative
    diagonal = level[3]
    step = resid / (middle * diagonal)
    field = jnp.zeros_like(step)
    for sweep_index in range(sweeps):
        field = field + step
        resid = resid - apply_whole(step, level)
        if sweep_index < sweeps - 1:
            ratio_next = 1.0 / (2.0 * relative - ratio_now)
            step = ratio_next * ratio_now * step + (2.0 * ratio_next / radius) * (resid / diagonal)
            ratio_now = ratio_next
    return field, resid


def reference(body_force, phase, viscosity_table, wall_kinds):
    viscosity = viscosity_table[phase]
    levels = []
    for level_index in range(LEVELS):
        levels.append(build_whole(viscosity, wall_kinds, 0.25 ** level_index))
        if level_index < LEVELS - 1:
            viscosity = halve(viscosity)
    resid = body_force
    fields = []
    resids = []
    for level_index in range(LEVELS - 1):
        field, resid = smooth_whole(resid, levels[level_index], fine_low, fine_high, SWEEPS)
        fields.append(field)
        resids.append(resid)
        resid = halve(resid)
    correction, unused = smooth_whole(resid, levels[LEVELS - 1], coarse_low, coarse_high, CSWEEPS)
    for level_index in reversed(range(LEVELS - 1)):
        lifted = widen(correction)
        resid = resids[level_index] - apply_whole(lifted, levels[level_index])
        extra, resid = smooth_whole(resid, levels[level_index], fine_low, fine_high, SWEEPS)
        correction = fields[level_index] + lifted + extra
    return levels[0][3] * correction, resid
```

```python
import jax
import jax.numpy as jnp
from jax import lax
from jax.experimental import pallas as pl
from jax.experimental.pallas import tpu as pltpu
from jax.sharding import PartitionSpec as P


F32 = jnp.float32
MESH = pl.DeviceIdType.MESH
LEVELS = 4
CSWEEPS = 24
NX = 32
NY = 8
LOW, HIGH = 0.2, 2.0
CLOW, CHIGH = 0.05, 2.0

MID = (HIGH + LOW) / 2.0
RAD = (HIGH - LOW) / 2.0
SIG = MID / RAD
RHO0 = 1.0 / SIG
RHO1 = 1.0 / (2.0 * SIG - RHO0)
STEP_A = RHO1 * RHO0
STEP_B = 2.0 * RHO1 / RAD

CMID = (CHIGH + CLOW) / 2.0
CRAD = (CHIGH - CLOW) / 2.0
CSIG = CMID / CRAD

SIDES = [(dx, dy) for dx in (-1, 0, 1) for dy in (-1, 0, 1) if dx or dy]
PAD = 4
BLOCK = 4
CHUNK = 8


def lanes():
    return lax.broadcasted_iota(jnp.int32, (8, 128), 1)


def subs():
    return lax.broadcasted_iota(jnp.int32, (8, 128), 0)


def tiled(index, values):
    return jnp.broadcast_to(index, values.shape)


def roll_lane(values, shift):
    return pltpu.roll(values, shift % 128, values.ndim - 1)


def roll_sub(values, shift):
    return pltpu.roll(values, shift % 8, values.ndim - 2)


def pick_lane(values, index):
    return jnp.take_along_axis(values, tiled(index, values), axis=values.ndim - 1, mode="promise_in_bounds")


def choose(mask, one, other):
    return jnp.where(tiled(mask, one), one, other)


def above(values, reach):
    moved = roll_lane(values, -reach)
    return choose(lanes() >= 128 - reach, roll_sub(moved, -1), moved)


def below(values, reach):
    moved = roll_lane(values, reach)
    return choose(lanes() < reach, roll_sub(moved, 1), moved)


def pair_sum(values, reach):
    return values + choose((lanes() & reach) == 0, roll_lane(values, -reach), roll_lane(values, reach))


def spread_sub(values, group):
    kept = jnp.where(tiled(subs() // 2 == group, values), values, 0.0)
    kept = kept + roll_sub(kept, 2)
    return kept + roll_sub(kept, 4)


def by_group(parts):
    group = subs() // 2
    out = parts[3]
    for k in (2, 1, 0):
        out = choose(group == k, parts[k], out)
    return out


def quad(lo, hi):
    return [(j, min(CHUNK, hi - j)) for j in range(lo, hi, CHUNK)]


def loop(lo, hi, body):
    def step(i, carry):
        body(i)
        return carry

    lax.fori_loop(lo, hi, step, 0)


class Level:
    def __init__(self, index, block, halo, refs):
        self.block, self.halo = block, halo
        self.frame = block + 2 * halo
        self.reach = 2**index
        self.scale = 0.25**index
        self.V, self.KX, self.KY, self.KZ, self.D, self.I, self.R, self.SA, self.SB, self.Q, self.X, self.PR = refs

    def near(self, ref, i, j, m):
        wide = ref[i, pl.ds(j - 1, m + 2)]
        mid = wide[1:-1]
        ky = self.KY[i, pl.ds(j, m + 1)]
        kz = self.KZ[i, pl.ds(j, m)]
        out = self.KX[i, pl.ds(j, m)] * ref[i - 1, pl.ds(j, m)]
        out = out + self.KX[i + 1, pl.ds(j, m)] * ref[i + 1, pl.ds(j, m)]
        out = out + (ky[:-1] * wide[:-2] + ky[1:] * wide[2:])
        out = out + (kz * above(mid, self.reach) + below(kz * mid, self.reach))
        return mid, out

    def build(self, gx, gy, kinds, lo, hi):
        h, b = self.halo, self.block
        half = 0.5 * self.scale
        group, side = subs() // 2, subs() % 2

        def per_kind(wall):
            tile = jnp.zeros((8, 128), F32)
            for c in range(3):
                tile = jnp.where(group == c, kinds[c, wall].astype(F32), tile)
            return tile

        walls = [per_kind(wall) for wall in range(6)]
        z_low = (side == 0) & (lanes() < self.reach)
        z_high = (side == 1) & (lanes() >= 128 - self.reach)
        z_wall = jnp.where(z_low, walls[4], 0.0) + jnp.where(z_high, walls[5], 0.0)
        one, zero = jnp.float32(1.0), jnp.float32(0.0)
        at_x = (jnp.where(gx == 0, one, zero), jnp.where(gx == NX - 1, one, zero))
        at_y = (jnp.where(gy == 0, one, zero), jnp.where(gy == NY - 1, one, zero))

        def faces(i):
            place = gx * b + i - h
            open_x = jnp.where((place == 0) | (place == NX * b), zero, one)
            for j, m in quad(lo, hi):
                here = self.V[i, pl.ds(j, m)]
                self.KX[i, pl.ds(j, m)] = (half * open_x) * (self.V[i - 1, pl.ds(j, m)] + here)

        loop(lo, hi + 1, faces)

        def rest(i):
            x_wall = z_wall + jnp.where(i == h, at_x[0], zero) * walls[0]
            x_wall = x_wall + jnp.where(i == h + b - 1, at_x[1], zero) * walls[1]
            for j, m in quad(lo, hi + 1):
                self.KY[i, pl.ds(j, m)] = half * (self.V[i, pl.ds(j - 1, m)] + self.V[i, pl.ds(j, m)])
            self.KY[i, h] = self.KY[i, h] * (one - at_y[0])
            self.KY[i, h + b] = self.KY[i, h + b] * (one - at_y[1])
            for j, m in quad(lo, hi):
                here = self.V[i, pl.ds(j, m)]
                ky = self.KY[i, pl.ds(j, m + 1)]
                kz = half * (here + above(here, self.reach))
                kz = jnp.where(tiled(z_high, kz), 0.0, kz)
                self.KZ[i, pl.ds(j, m)] = kz
                total = self.KX[i, pl.ds(j, m)] + self.KX[i + 1, pl.ds(j, m)] + (ky[:-1] + ky[1:])
                total = total + (kz + below(kz, self.reach))
                self.D[i, pl.ds(j, m)] = total + (2.0 * self.scale) * here * tiled(x_wall, here)
            for j, wall, at in ((h, walls[2], at_y[0]), (h + b - 1, walls[3], at_y[1])):
                self.D[i, j] = self.D[i, j] + (2.0 * self.scale * at) * self.V[i, j] * wall
            for j, m in quad(lo, hi):
                self.I[i, pl.ds(j, m)] = 1.0 / self.D[i, pl.ds(j, m)]

        loop(lo, hi, rest)

    def first_step(self, src, lo, hi):
        def body(i):
            for j, m in quad(lo, hi):
                self.SA[i, pl.ds(j, m)] = src[i, pl.ds(j, m)] * self.I[i, pl.ds(j, m)] * (1.0 / MID)

        loop(lo, hi, body)

    def second_step(self, src, dst, lo, hi):
        def body(i):
            for j, m in quad(lo, hi):
                step, near = self.near(self.SA, i, j, m)
                r = src[i, pl.ds(j, m)] * (1.0 - 1.0 / MID) + near
                dst[i, pl.ds(j, m)] = r
                self.SB[i, pl.ds(j, m)] = STEP_A * step + STEP_B * (r * self.I[i, pl.ds(j, m)])

        loop(lo, hi, body)

    def descend(self):
        h, b = self.halo, self.block
        self.first_step(self.R, h - 2, h + b + 2)
        self.second_step(self.R, self.Q, h - 1, h + b + 1)

        def body(i):
            for j, m in quad(h, h + b):
                step, near = self.near(self.SB, i, j, m)
                self.Q[i, pl.ds(j, m)] = self.Q[i, pl.ds(j, m)] - self.D[i, pl.ds(j, m)] * step + near
                self.X[i, pl.ds(j, m)] = self.SA[i, pl.ds(j, m)] + step

        loop(h, h + b, body)

    def lift(self, ref, shift, first, count):
        def body(i):
            row = ref[(i + shift[0]) // 2 + shift[1], pl.ds(first, count)]
            row = jnp.broadcast_to(row[:, None], (count, 2, 8, 128)).reshape(2 * count, 8, 128)
            skip = (2 * count - self.frame) // 2
            self.PR[i] = row[skip : skip + self.frame]

        loop(0, self.frame, body)

    def correct(self, lo, hi):
        def body(i):
            for j, m in quad(lo, hi):
                lifted, near = self.near(self.PR, i, j, m)
                q = self.Q[i, pl.ds(j, m)] - self.D[i, pl.ds(j, m)] * lifted + near
                self.R[i, pl.ds(j, m)] = q
                self.SA[i, pl.ds(j, m)] = q * self.I[i, pl.ds(j, m)] * (1.0 / MID)

        loop(lo, hi, body)


def halo_copies(ref, own, halo, cut, gx, gy, send, recv, first):
    copies = []
    for k, (dx, dy) in enumerate(SIDES):
        src, dst = [], []
        for d, o, h, w in ((dx, own[0], halo[0], cut[0]), (dy, own[1], halo[1], cut[1])):
            if d == 0:
                src.append(pl.ds(h, o))
                dst.append(pl.ds(h, o))
            elif d < 0:
                src.append(pl.ds(h, w))
                dst.append(pl.ds(h + o, w))
            else:
                src.append(pl.ds(h + o - w, w))
                dst.append(pl.ds(h - w, w))
        target = (lax.rem(gx + dx + NX, NX), lax.rem(gy + dy + NY, NY))
        copies.append(
            pltpu.make_async_remote_copy(
                src_ref=ref.at[src[0], src[1]],
                dst_ref=ref.at[dst[0], dst[1]],
                send_sem=send.at[first + k],
                recv_sem=recv.at[first + k],
                device_id=target,
                device_id_type=MESH,
            )
        )
    return copies


def kernel(
    force, phase, table, kinds, out_w, out_r,
    PH, RP1, VP1, QP1, XP1, RP2, VP2, QP2, XP2, MSG, CG, CR, CV, KXM, KXP, KA, KB, KZ, CD, CI, CS, CE, OW, *rest,
):
    refs0, refs1, refs2 = rest[0:12], rest[12:24], rest[24:36]
    in_sem, send, recv = rest[36:]
    gx, gy = lax.axis_index("gx"), lax.axis_index("gy")
    core = lax.rem(gx, 2)
    pair = gx // 2
    L0, L1, L2 = Level(0, 16, 3, refs0), Level(1, 8, 4, refs1), Level(2, 4, 4, refs2)
    group, side, lane = subs() // 2, subs() % 2, lanes()

    loads = []
    for c in range(3):
        for s in range(2):
            loads.append(
                pltpu.make_async_copy(
                    force.at[c, :, :, pl.ds(128 * s, 128)],
                    L0.R.at[pl.ds(3, 16), pl.ds(3, 16), 2 * c + s],
                    in_sem.at[len(loads)],
                )
            )
    for c in range(4):
        for s in range(2):
            loads.append(
                pltpu.make_async_copy(
                    phase.at[:, :, pl.ds(128 * s, 128)], PH.at[:, :, 2 * c + s], in_sem.at[len(loads)]
                )
            )
    for copy in loads:
        copy.start()

    partners = [(lax.rem(gx + dx + NX, NX), lax.rem(gy + dy + NY, NY)) for dx, dy in SIDES]
    partners += [(gx, lax.rem(gy + k, NY)) for k in range(2, 7)]
    partners += [(lax.rem(gx + 2 * k, NX), gy) for k in range(1, 16)]
    barrier = pltpu.get_barrier_semaphore()
    for partner in partners:
        pl.semaphore_signal(barrier, inc=1, device_id=partner, device_id_type=MESH)

    values = jnp.zeros((8, 128), F32)
    for k in range(8):
        values = jnp.where(lane == k, table[k], values)
    for copy in loads:
        copy.wait()

    def look_up(i):
        for j, m in quad(0, 16):
            index = PH[i, pl.ds(j, m)]
            cells = pick_lane(jnp.broadcast_to(values, index.shape), index)
            L0.V[i + 3, pl.ds(j + 3, m)] = cells
            L0.R[i + 3, pl.ds(j + 3, m)] = choose(group == 3, cells, L0.R[i + 3, pl.ds(j + 3, m)])

    loop(0, 16, look_up)
    pl.semaphore_wait(barrier, len(partners))

    pending = halo_copies(L0.R, (16, 16), (3, 3), (2, 2), gx, gy, send, recv, 0)
    for k, (dx, dy) in enumerate(((-1, 0), (1, 0), (0, -1), (0, 1))):
        span = {0: (pl.ds(3, 16), pl.ds(3, 16)), -1: (pl.ds(5, 1), pl.ds(21, 1)), 1: (pl.ds(16, 1), pl.ds(0, 1))}
        pending.append(
            pltpu.make_async_remote_copy(
                src_ref=L0.R.at[span[dx][0], span[dy][0], pl.ds(6, 2)],
                dst_ref=L0.R.at[span[dx][1], span[dy][1], pl.ds(6, 2)],
                send_sem=send.at[8 + k],
                recv_sem=recv.at[8 + k],
                device_id=(lax.rem(gx + dx + NX, NX), lax.rem(gy + dy + NY, NY)),
                device_id_type=MESH,
            )
        )
    for copy in pending:
        copy.start()
    faces = pending
    sent = []

    def restrict(src, halo_src, count, reach, i):
        row = src[halo_src + 2 * i, pl.ds(halo_src, count)] + src[halo_src + 2 * i + 1, pl.ds(halo_src, count)]
        row = row.reshape(count // 2, 2, 8, 128)
        return pair_sum(row[:, 0] + row[:, 1], reach) * 0.125

    def coarsen_v1(i):
        L1.V[4 + i, pl.ds(4, 8)] = restrict(L0.V, 3, 16, 1, i)

    def coarsen_v2(i):
        L2.V[4 + i, pl.ds(4, 4)] = restrict(L1.V, 4, 8, 2, i)

    loop(0, 8, coarsen_v1)
    loop(0, 4, coarsen_v2)

    def pack_v1(a):
        for b in range(2):
            parts = [by_group([L1.V[4 + 2 * a + p, 4 + 4 * b + k] for k in range(4)]) for p in range(2)]
            VP1[a + 2, b + 1] = jnp.where(lane % 2 == 0, parts[0], parts[1])

    loop(0, 4, pack_v1)
    tile = None
    for p in range(4):
        part = by_group([L2.V[4 + p, 4 + k] for k in range(4)])
        tile = part if tile is None else jnp.where(lane % 4 == p, part, tile)
    VP2[1, 1] = tile

    for copy in pending:
        copy.wait_recv()

    early = halo_copies(VP1, (4, 2), (2, 1), (2, 1), gx, gy, send, recv, 12)
    early += halo_copies(VP2, (1, 1), (1, 1), (1, 1), gx, gy, send, recv, 20)
    for copy in early:
        copy.start()
    sent += early

    def fill_v0(i):
        for j, m in quad(0, 22):
            L0.V[i, pl.ds(j, m)] = spread_sub(L0.R[i, pl.ds(j, m)], 3)

    loop(0, 22, fill_v0)
    L0.build(gx, gy, kinds, 1, 21)
    L0.descend()
    for copy in faces:
        copy.wait_send()

    def pack_r1(a):
        one, other = restrict(L0.Q, 3, 16, 1, 2 * a), restrict(L0.Q, 3, 16, 1, 2 * a + 1)
        RP1[a + 1, pl.ds(2, 8)] = choose(lane % 2 == 0, one, other)

    loop(0, 4, pack_r1)
    pending = halo_copies(RP1, (4, 8), (1, 2), (1, 2), gx, gy, send, recv, 28)
    for copy in pending:
        copy.start()
    sent += pending
    for copy in early:
        copy.wait_recv()

    def unpack_v1(a):
        for b in range(4):
            both = VP1[a, b]
            for p in range(2):
                part = pick_lane(both, (lane // 2) * 2 + p)
                for k in range(4):
                    L1.V[2 * a + p, 4 * b + k] = spread_sub(part, k)

    loop(0, 8, unpack_v1)

    def unpack_v2(a):
        for b in range(3):
            both = VP2[a, b]
            for p in range(4):
                part = pick_lane(both, (lane // 4) * 4 + p)
                for k in range(4):
                    L2.V[4 * a + p, 4 * b + k] = spread_sub(part, k)

    loop(0, 3, unpack_v2)
    L1.build(gx, gy, kinds, 1, 15)
    L2.build(gx, gy, kinds, 1, 11)
    for copy in pending:
        copy.wait_recv()

    def unpack_pairs(src, dst, count, x_first, y_first, y_count):
        def body(a):
            row = src[a, pl.ds(0, y_count)]
            for p in range(2):
                dst[x_first + 2 * a + p, pl.ds(y_first, y_count)] = pick_lane(row, (lane // 2) * 2 + p)

        loop(0, count, body)

    unpack_pairs(RP1, L1.R, 6, 2, 2, 12)
    L1.descend()

    def pack_r2(a):
        rows = []
        for p in range(2):
            row = restrict(L1.Q, 4, 8, 2, 2 * a + p).reshape(2, 2, 8, 128)
            rows.append(choose(lane % 2 == 0, row[:, 0], row[:, 1]))
        RP2[a + 1, pl.ds(1, 2)] = choose(lane % 4 < 2, rows[0], rows[1])

    loop(0, 2, pack_r2)
    pending = halo_copies(RP2, (2, 2), (1, 1), (1, 1), gx, gy, send, recv, 36)
    for copy in pending:
        copy.start()
    sent += pending
    for copy in pending:
        copy.wait_recv()

    def unpack_quads(src, dst, count, first):
        def body(a):
            for b in range(count):
                both = src[a, b]
                for p in range(2):
                    for k in range(2):
                        dst[first + 2 * a + p, first + 2 * b + k] = pick_lane(both, (lane // 4) * 4 + (2 * p + k))

        loop(0, count, body)

    unpack_quads(RP2, L2.R, 4, 2)
    L2.descend()

    for p in range(2):
        r3 = restrict(L2.Q, 4, 4, 4, p)
        v3 = restrict(L2.V, 4, 4, 4, p)
        both = choose(group == 3, v3, r3)
        both = pick_lane(both, 8 * (lane % 16))
        both = jnp.where(tiled(lane // 16 == subs(), both), both, 0.0)
        for k in range(2):
            MSG[pl.ds(2 * p + k, 1), :] = jnp.sum(both[k], axis=0, keepdims=True)
    rows = pl.ds(pl.multiple_of(4 * gy, 4), 4)
    keep = pltpu.make_async_copy(MSG.at[pl.ds(0, 4)], CG.at[pair, core, rows], in_sem.at[0])
    keep.start()
    pending = []
    for k in range(1, 16):
        pending.append(
            pltpu.make_async_remote_copy(
                src_ref=MSG.at[pl.ds(0, 4)],
                dst_ref=CG.at[pair, core, rows],
                send_sem=send.at[44 + k - 1],
                recv_sem=recv.at[44 + k - 1],
                device_id=(lax.rem(gx + 2 * k, NX), gy),
                device_id_type=MESH,
            )
        )
    for copy in pending:
        copy.start()
    sent += pending

    def pack_1(a):
        for src, dst, x0, y0 in ((L1.Q, QP1, 2, 3), (L1.X, XP1, 1, 2)):
            one, other = src[4 + 2 * a, pl.ds(4, 8)], src[5 + 2 * a, pl.ds(4, 8)]
            dst[x0 + a, pl.ds(y0, 8)] = choose(lane % 2 == 0, one, other)

    loop(0, 4, pack_1)

    def pack_2(a):
        for src, dst, x0 in ((L2.Q, QP2, 2), (L2.X, XP2, 1)):
            mixed = []
            for p in range(2):
                row = src[4 + 2 * a + p, pl.ds(4, 4)].reshape(2, 2, 8, 128)
                mixed.append(choose(lane % 2 == 0, row[:, 0], row[:, 1]))
            dst[x0 + a, pl.ds(x0, 2)] = choose(lane % 4 < 2, mixed[0], mixed[1])

    loop(0, 2, pack_2)
    keep.wait()
    for copy in pending:
        copy.wait_recv()

    pending = []
    for k in range(1, 8):
        pending.append(
            pltpu.make_async_remote_copy(
                src_ref=CG.at[:, core, rows],
                dst_ref=CG.at[:, core, rows],
                send_sem=send.at[59 + k - 1],
                recv_sem=recv.at[59 + k - 1],
                device_id=(gx, lax.rem(gy + k, NY)),
                device_id_type=MESH,
            )
        )
    for copy in pending:
        copy.start()
    sent += pending
    for copy in pending:
        copy.wait_recv()
    swap = pltpu.make_async_remote_copy(
        src_ref=CG.at[:, core],
        dst_ref=CG.at[:, core],
        send_sem=send.at[66],
        recv_sem=recv.at[66],
        device_id=(gx + 1 - 2 * core, gy),
        device_id_type=MESH,
    )
    swap.start()
    sent.append(swap)
    late2 = halo_copies(QP2, (2, 2), (2, 2), (2, 2), gx, gy, send, recv, 67)
    late2 += halo_copies(XP2, (2, 2), (1, 1), (1, 1), gx, gy, send, recv, 75)
    late1 = halo_copies(QP1, (4, 8), (2, 3), (2, 3), gx, gy, send, recv, 83)
    late1 += halo_copies(XP1, (4, 8), (1, 2), (1, 2), gx, gy, send, recv, 91)
    late0 = halo_copies(L0.Q, (16, 16), (3, 3), (2, 2), gx, gy, send, recv, 99)
    swap.wait_recv()
    for copy in late2 + late1 + late0:
        copy.start()
    sent += late2 + late1 + late0

    coarse(gx, gy, kinds, CG, CR, CV, KXM, KXP, KA, KB, KZ, CD, CI, CS, CE)

    flat = CE.reshape(96, 128)

    def expand(a):
        for j in range(6):
            row = 16 * a + 8 * (j % 2) + lax.rem(gy + 7 + j // 2, 8)
            both = jnp.broadcast_to(flat[pl.ds(row, 1), :], (8, 128))
            both = pick_lane(both, 16 * subs() + lane // 8)
            for p in range(2):
                for k in range(2):
                    L2.PR[2 * a + p, 2 * j + k] = both

    loop(0, 6, expand)

    for copy in late2:
        copy.wait_recv()
    unpack_quads(QP2, L2.Q, 6, 0)
    unpack_quads(XP2, L2.X, 4, 2)

    def middle(level):
        h, b = level.halo, level.block
        level.correct(h - 3, h + b + 3)
        level.second_step(level.R, level.R, h - 2, h + b + 2)

        def body(i):
            for j, m in quad(h - 2, h + b + 2):
                here = pl.ds(j, m)
                level.SB[i, here] = (level.X[i, here] + level.PR[i, here]) + (level.SA[i, here] + level.SB[i, here])

        loop(h - 2, h + b + 2, body)

    middle(L2)
    L1.lift(L2.SB, (0, 2), 2, 8)
    for copy in late1:
        copy.wait_recv()

    def unpack_q1(a):
        row = QP1[a]
        for p in range(2):
            L1.Q[2 * a + p, pl.ds(1, 14)] = pick_lane(row, (lane // 2) * 2 + p)

    loop(0, 8, unpack_q1)
    unpack_pairs(XP1, L1.X, 6, 2, 2, 12)
    middle(L1)
    L0.lift(L1.SB, (1, 2), 2, 12)
    for copy in late0:
        copy.wait_recv()
    L0.correct(1, 21)
    L0.second_step(L0.R, L0.R, 2, 20)

    def last(i):
        for j, m in quad(3, 19):
            here = pl.ds(j, m)
            step, near = L0.near(L0.SB, i, j, m)
            diag = L0.D[i, here]
            field = (L0.X[i, here] + L0.PR[i, here]) + (L0.SA[i, here] + step)
            L0.R[i, here] = L0.R[i, here] - diag * step + near
            OW[i - 3, pl.ds(j - 3, m)] = diag * field

    loop(3, 19, last)
    stores = []
    for c in range(3):
        for s in range(2):
            place = pl.ds(128 * s, 128)
            stores.append(
                pltpu.make_async_copy(OW.at[:, :, 2 * c + s], out_w.at[c, :, :, place], in_sem.at[len(stores)])
            )
            stores.append(
                pltpu.make_async_copy(
                    L0.R.at[pl.ds(3, 16), pl.ds(3, 16), 2 * c + s],
                    out_r.at[c, :, :, place],
                    in_sem.at[len(stores)],
                )
            )
    for copy in stores:
        copy.start()
    for copy in sent:
        copy.wait_send()
    for copy in stores:
        copy.wait()


def coarse(gx, gy, kinds, CG, CR, CV, KXM, KXP, KA, KB, KZ, CD, CI, CS, CE):
    planes = 2 * NX
    scale = 0.25 ** (LEVELS - 1)
    lane = lanes()
    spot = lane % 32
    flat = CG.reshape(1024, 128)

    def blocks(reach, body):
        lo = jnp.maximum(2 * gx - 2 - reach, 0) // BLOCK
        hi = (jnp.minimum(2 * gx + 4 + reach, planes) + BLOCK - 1) // BLOCK
        loop(lo, hi, body)

    zeros = jnp.zeros((PAD, 2, 8, 128), F32)
    for place in (0, PAD + planes):
        CV[pl.ds(place, PAD)] = zeros
        CS[0, pl.ds(place, PAD)] = zeros
        CS[1, pl.ds(place, PAD)] = zeros

    def take(b):
        for q in range(BLOCK):
            for y in range(2):
                start = 128 * b // 2 + 32 * (q // 2) + 2 * (q % 2) + y
                row = flat[pl.ds(start, 8, stride=4), :]
                CR[PAD + BLOCK * b + q, y] = row
                CV[PAD + BLOCK * b + q, y] = pick_lane(row, 96 + spot)

    blocks(26, take)

    def per_kind(wall):
        tile = jnp.zeros((8, 128), F32)
        for c in range(3):
            tile = jnp.where(lane // 32 == c, kinds[c, wall].astype(F32), tile)
        return tile

    walls = [per_kind(wall) for wall in range(6)]
    z_wall = jnp.where(spot == 0, walls[4], 0.0) + jnp.where(spot == 31, walls[5], 0.0)
    low_y = z_wall + jnp.where(subs() == 0, walls[2], 0.0)
    high_y = z_wall + jnp.where(subs() == 7, walls[3], 0.0)

    def setup(b):
        here = pl.ds(PAD + BLOCK * b, BLOCK)
        prev, after = pl.ds(PAD - 1 + BLOCK * b, BLOCK), pl.ds(PAD + 1 + BLOCK * b, BLOCK)
        plane = lax.broadcasted_iota(jnp.int32, (BLOCK, 8, 128), 0) + BLOCK * b
        even, odd = CV[here, 0], CV[here, 1]
        half = 0.5 * scale
        ka = half * (even + odd)
        kb = half * (odd + roll_sub(even, -1))
        kb = jnp.where(tiled(subs() == 7, kb), 0.0, kb)
        KA[here] = ka
        KB[here] = kb
        x_wall = jnp.where(plane == 0, tiled(walls[0], even), 0.0)
        x_wall = x_wall + jnp.where(plane == planes - 1, tiled(walls[1], even), 0.0)
        for y, value, wall, other in ((0, even, low_y, roll_sub(kb, 1)), (1, odd, high_y, kb)):
            kxm = jnp.where(plane == 0, 0.0, half * (CV[prev, y] + value))
            kxp = jnp.where(plane == planes - 1, 0.0, half * (value + CV[after, y]))
            kz = half * (value + roll_lane(value, -1))
            kz = jnp.where(tiled(spot == 31, kz), 0.0, kz)
            KXM[here, y] = kxm
            KXP[here, y] = kxp
            KZ[here, y] = kz
            total = (kxm + kxp) + (ka + other) + (kz + roll_lane(kz, 1))
            total = total + (2.0 * scale) * value * (x_wall + tiled(wall, value))
            CD[here, y] = total
            inverse = 1.0 / total
            CI[here, y] = inverse
            CS[0, here, y] = CR[here, y] * inverse * (1.0 / CMID)

    blocks(25, setup)

    own = pl.ds(PAD - 2 + 2 * gx, 6)
    CE[...] = CS[0, own]

    def sweep(k, rho):
        now, later = lax.rem(k, 2), lax.rem(k + 1, 2)
        rho_next = 1.0 / (2.0 * CSIG - rho)
        step_a = rho_next * rho
        step_b = rho_next * (2.0 / CRAD)

        def body(b):
            here = pl.ds(PAD + BLOCK * b, BLOCK)
            prev, after = pl.ds(PAD - 1 + BLOCK * b, BLOCK), pl.ds(PAD + 1 + BLOCK * b, BLOCK)
            even, odd = CS[now, here, 0], CS[now, here, 1]
            ka, kb = KA[here], KB[here]
            for y, value, beside in (
                (0, even, ka * odd + roll_sub(kb * odd, 1)),
                (1, odd, ka * even + kb * roll_sub(even, -1)),
            ):
                kz = KZ[here, y]
                near = KXM[here, y] * CS[now, prev, y] + KXP[here, y] * CS[now, after, y] + beside
                near = near + (kz * roll_lane(value, -1) + roll_lane(kz * value, 1))
                r = CR[here, y] - CD[here, y] * value + near
                CR[here, y] = r
                CS[later, here, y] = tiled(step_a, r) * value + tiled(step_b, r) * (r * CI[here, y])

        blocks(CSWEEPS - 2 - k, body)
        CE[...] = CE[...] + CS[later, own]
        return rho_next

    lax.fori_loop(0, CSWEEPS - 1, sweep, jnp.full((8, 128), 1.0 / CSIG, F32))


def per_device(body_force, phase, viscosity_table, wall_kinds):
    def vmem(*lead):
        return pltpu.VMEM(lead + (8, 128), F32)

    scratch = [
        pltpu.VMEM((16, 16, 8, 128), jnp.int32),
        vmem(6, 12), vmem(8, 4), vmem(8, 14), vmem(6, 12),
        vmem(4, 4), vmem(3, 3), vmem(6, 6), vmem(4, 4),
        vmem(), pltpu.VMEM((16, 2, 32, 128), F32),
    ]
    depth = 2 * NX + 2 * PAD
    scratch += [vmem(depth, 2)] * 4 + [vmem(depth)] * 2 + [vmem(depth, 2)] * 3 + [vmem(2, depth, 2), vmem(6, 2)]
    scratch += [vmem(16, 16)]
    for frame in (22, 16, 12):
        scratch += [vmem(frame, frame)] * 12
    n_sems = 107
    scratch += [pltpu.SemaphoreType.DMA((14,)), pltpu.SemaphoreType.DMA((n_sems,)), pltpu.SemaphoreType.DMA((n_sems,))]
    shape = jax.ShapeDtypeStruct(body_force.shape, F32)
    return pl.pallas_call(
        kernel,
        out_shape=(shape, shape),
        in_specs=[
            pl.BlockSpec(memory_space=pl.ANY),
            pl.BlockSpec(memory_space=pl.ANY),
            pl.BlockSpec(memory_space=pltpu.SMEM),
            pl.BlockSpec(memory_space=pltpu.SMEM),
        ],
        out_specs=(pl.BlockSpec(memory_space=pl.ANY), pl.BlockSpec(memory_space=pl.ANY)),
        scratch_shapes=scratch,
        compiler_params=pltpu.CompilerParams(
            collective_id=0, has_side_effects=True, vmem_limit_bytes=56 * 2**20
        ),
        name="vcycle",
    )(body_force, phase, viscosity_table, wall_kinds)


def solution(mesh):
    placed = (P(None, "gx", "gy", None), P("gx", "gy", None), P(), P())
    return jax.shard_map(
        per_device,
        mesh=mesh,
        in_specs=placed,
        out_specs=(P(None, "gx", "gy", None), P(None, "gx", "gy", None)),
        check_vma=False,
    )
```

```python
import jax
import jax.numpy as jnp
from jax import lax
from jax.experimental import pallas as pl
from jax.experimental.pallas import tpu as pltpu
from jax.sharding import PartitionSpec as P


F32 = jnp.float32
MESH = pl.DeviceIdType.MESH
LEVELS = 4
CSWEEPS = 24
NX = 32
NY = 8
LOW, HIGH = 0.2, 2.0
CLOW, CHIGH = 0.05, 2.0

MID = (HIGH + LOW) / 2.0
RAD = (HIGH - LOW) / 2.0
SIG = MID / RAD
RHO0 = 1.0 / SIG
RHO1 = 1.0 / (2.0 * SIG - RHO0)
STEP_A = RHO1 * RHO0
STEP_B = 2.0 * RHO1 / RAD

CMID = (CHIGH + CLOW) / 2.0
CRAD = (CHIGH - CLOW) / 2.0
CSIG = CMID / CRAD

SIDES = [(dx, dy) for dx in (-1, 0, 1) for dy in (-1, 0, 1) if dx or dy]
PAD = 4
BLOCK = 16
CHUNK = 8


def lanes():
    return lax.broadcasted_iota(jnp.int32, (8, 128), 1)


def subs():
    return lax.broadcasted_iota(jnp.int32, (8, 128), 0)


def tiled(index, values):
    return jnp.broadcast_to(index, values.shape)


def roll_lane(values, shift):
    return pltpu.roll(values, shift % 128, values.ndim - 1)


def roll_sub(values, shift):
    return pltpu.roll(values, shift % 8, values.ndim - 2)


def pick_lane(values, index):
    return jnp.take_along_axis(values, tiled(index, values), axis=values.ndim - 1, mode="promise_in_bounds")


def choose(mask, one, other):
    return jnp.where(tiled(mask, one), one, other)


def above(values, reach):
    moved = roll_lane(values, -reach)
    return choose(lanes() >= 128 - reach, roll_sub(moved, -1), moved)


def below(values, reach):
    moved = roll_lane(values, reach)
    return choose(lanes() < reach, roll_sub(moved, 1), moved)


def pair_sum(values, reach):
    return values + choose((lanes() & reach) == 0, roll_lane(values, -reach), roll_lane(values, reach))


def spread_sub(values, group):
    kept = jnp.where(tiled(subs() // 2 == group, values), values, 0.0)
    kept = kept + roll_sub(kept, 2)
    return kept + roll_sub(kept, 4)


def by_group(parts):
    group = subs() // 2
    out = parts[3]
    for k in (2, 1, 0):
        out = choose(group == k, parts[k], out)
    return out


def quad(lo, hi):
    return [(j, min(CHUNK, hi - j)) for j in range(lo, hi, CHUNK)]


def loop(lo, hi, body):
    whole = isinstance(lo, int) and isinstance(hi, int)
    turns = next(k for k in (4, 3, 2, 1) if k == 1 or whole and (hi - lo) % k == 0)

    def step(t, carry):
        for k in range(turns):
            body(lo + turns * t + k)
        return carry

    lax.fori_loop(0, (hi - lo) // turns, step, 0)


def clear(ref):
    rows, columns = ref.shape[:2]

    def body(i):
        ref[i] = jnp.zeros((columns, 8, 128), F32)

    loop(0, rows, body)


class Level:
    def __init__(self, index, block, halo, refs):
        self.block, self.halo = block, halo
        self.frame = block + 2 * halo
        self.reach = 2**index
        self.scale = 0.25**index
        self.V, self.KX, self.KY, self.KZ, self.D, self.I, self.R, self.SA, self.SB, self.Q, self.X, self.PR = refs

    def near(self, ref, i, j, m):
        wide = ref[i, pl.ds(j - 1, m + 2)]
        mid = wide[1:-1]
        ky = self.KY[i, pl.ds(j, m + 1)]
        kz = self.KZ[i, pl.ds(j, m)]
        out = self.KX[i, pl.ds(j, m)] * ref[i - 1, pl.ds(j, m)]
        out = out + self.KX[i + 1, pl.ds(j, m)] * ref[i + 1, pl.ds(j, m)]
        out = out + (ky[:-1] * wide[:-2] + ky[1:] * wide[2:])
        out = out + (kz * above(mid, self.reach) + below(kz * mid, self.reach))
        return mid, out

    def build(self, gx, gy, kinds, lo, hi):
        h, b = self.halo, self.block
        half = 0.5 * self.scale
        group, side = subs() // 2, subs() % 2

        def per_kind(wall):
            tile = jnp.zeros((8, 128), F32)
            for c in range(3):
                tile = jnp.where(group == c, kinds[c, wall].astype(F32), tile)
            return tile

        walls = [per_kind(wall) for wall in range(6)]
        z_low = (side == 0) & (lanes() < self.reach)
        z_high = (side == 1) & (lanes() >= 128 - self.reach)
        z_wall = jnp.where(z_low, walls[4], 0.0) + jnp.where(z_high, walls[5], 0.0)
        one, zero = jnp.float32(1.0), jnp.float32(0.0)
        at_x = (jnp.where(gx == 0, one, zero), jnp.where(gx == NX - 1, one, zero))
        at_y = (jnp.where(gy == 0, one, zero), jnp.where(gy == NY - 1, one, zero))

        def faces(i):
            place = gx * b + i - h
            open_x = jnp.where((place == 0) | (place == NX * b), zero, one)
            for j, m in quad(lo, hi):
                here = self.V[i, pl.ds(j, m)]
                self.KX[i, pl.ds(j, m)] = (half * open_x) * (self.V[i - 1, pl.ds(j, m)] + here)

        loop(lo, hi + 1, faces)

        def rest(i):
            x_wall = z_wall + jnp.where(i == h, at_x[0], zero) * walls[0]
            x_wall = x_wall + jnp.where(i == h + b - 1, at_x[1], zero) * walls[1]
            for j, m in quad(lo, hi + 1):
                self.KY[i, pl.ds(j, m)] = half * (self.V[i, pl.ds(j - 1, m)] + self.V[i, pl.ds(j, m)])
            self.KY[i, h] = self.KY[i, h] * (one - at_y[0])
            self.KY[i, h + b] = self.KY[i, h + b] * (one - at_y[1])
            for j, m in quad(lo, hi):
                here = self.V[i, pl.ds(j, m)]
                ky = self.KY[i, pl.ds(j, m + 1)]
                kz = half * (here + above(here, self.reach))
                kz = jnp.where(tiled(z_high, kz), 0.0, kz)
                self.KZ[i, pl.ds(j, m)] = kz
                total = self.KX[i, pl.ds(j, m)] + self.KX[i + 1, pl.ds(j, m)] + (ky[:-1] + ky[1:])
                total = total + (kz + below(kz, self.reach))
                self.D[i, pl.ds(j, m)] = total + (2.0 * self.scale) * here * tiled(x_wall, here)
            for j, wall, at in ((h, walls[2], at_y[0]), (h + b - 1, walls[3], at_y[1])):
                self.D[i, j] = self.D[i, j] + (2.0 * self.scale * at) * self.V[i, j] * wall
            for j, m in quad(lo, hi):
                self.I[i, pl.ds(j, m)] = 1.0 / self.D[i, pl.ds(j, m)]

        loop(lo, hi, rest)

    def first_step(self, src, lo, hi):
        def body(i):
            for j, m in quad(lo, hi):
                self.SA[i, pl.ds(j, m)] = src[i, pl.ds(j, m)] * self.I[i, pl.ds(j, m)] * (1.0 / MID)

        loop(lo, hi, body)

    def second_step(self, src, dst, lo, hi):
        def body(i):
            for j, m in quad(lo, hi):
                step, near = self.near(self.SA, i, j, m)
                r = src[i, pl.ds(j, m)] * (1.0 - 1.0 / MID) + near
                dst[i, pl.ds(j, m)] = r
                self.SB[i, pl.ds(j, m)] = STEP_A * step + STEP_B * (r * self.I[i, pl.ds(j, m)])

        loop(lo, hi, body)

    def descend(self):
        h, b = self.halo, self.block
        self.first_step(self.R, h - 2, h + b + 2)
        self.second_step(self.R, self.Q, h - 1, h + b + 1)

        def body(i):
            for j, m in quad(h, h + b):
                step, near = self.near(self.SB, i, j, m)
                self.Q[i, pl.ds(j, m)] = self.Q[i, pl.ds(j, m)] - self.D[i, pl.ds(j, m)] * step + near
                self.X[i, pl.ds(j, m)] = self.SA[i, pl.ds(j, m)] + step

        loop(h, h + b, body)

    def lift(self, ref, shift, first, count):
        def body(i):
            row = ref[(i + shift[0]) // 2 + shift[1], pl.ds(first, count)]
            row = jnp.broadcast_to(row[:, None], (count, 2, 8, 128)).reshape(2 * count, 8, 128)
            skip = (2 * count - self.frame) // 2
            self.PR[i] = row[skip : skip + self.frame]

        loop(0, self.frame, body)

    def correct(self, lo, hi):
        def body(i):
            for j, m in quad(lo, hi):
                lifted, near = self.near(self.PR, i, j, m)
                q = self.Q[i, pl.ds(j, m)] - self.D[i, pl.ds(j, m)] * lifted + near
                self.R[i, pl.ds(j, m)] = q
                self.SA[i, pl.ds(j, m)] = q * self.I[i, pl.ds(j, m)] * (1.0 / MID)

        loop(lo, hi, body)


def halo_copies(ref, own, halo, cut, corner, gx, gy, send, recv, first, height=6):
    copies = []
    for k, (dx, dy) in enumerate(SIDES):
        src, dst = [], []
        wide = corner if dx and dy else cut
        for d, o, h, w in ((dx, own[0], halo[0], wide[0]), (dy, own[1], halo[1], wide[1])):
            if d == 0:
                src.append(pl.ds(h, o))
                dst.append(pl.ds(h, o))
            elif d < 0:
                src.append(pl.ds(h, w))
                dst.append(pl.ds(h + o, w))
            else:
                src.append(pl.ds(h + o - w, w))
                dst.append(pl.ds(h - w, w))
        target = (lax.rem(gx + dx + NX, NX), lax.rem(gy + dy + NY, NY))
        copies.append(
            pltpu.make_async_remote_copy(
                src_ref=ref.at[src[0], src[1], pl.ds(0, height)],
                dst_ref=ref.at[dst[0], dst[1], pl.ds(0, height)],
                send_sem=send.at[first + k],
                recv_sem=recv.at[first + k],
                device_id=target,
                device_id_type=MESH,
            )
        )
    return copies


def kernel(
    force, phase, table, kinds, out_w, out_r,
    PH, RP1, VP1, QP1, XP1, RP2, VP2, QP2, XP2, MSG, CG, CR, CV, KXM, KXP, KA, KB, KZ, CD, CI, CS, CE, OW, *rest,
):
    refs0, refs1, refs2 = rest[0:12], rest[12:24], rest[24:36]
    in_sem, send, recv = rest[36:]
    gx, gy = lax.axis_index("gx"), lax.axis_index("gy")
    core = lax.rem(gx, 2)
    pair = gx // 2
    L0, L1, L2 = Level(0, 16, 3, refs0), Level(1, 8, 4, refs1), Level(2, 4, 4, refs2)
    group, side, lane = subs() // 2, subs() % 2, lanes()

    loads = []
    for c in range(3):
        for s in range(2):
            loads.append(
                pltpu.make_async_copy(
                    force.at[c, :, :, pl.ds(128 * s, 128)],
                    L0.R.at[pl.ds(3, 16), pl.ds(3, 16), 2 * c + s],
                    in_sem.at[len(loads)],
                )
            )
    for c in range(4):
        for s in range(2):
            loads.append(
                pltpu.make_async_copy(
                    phase.at[:, :, pl.ds(128 * s, 128)], PH.at[:, :, 2 * c + s], in_sem.at[len(loads)]
                )
            )
    for copy in loads:
        copy.start()

    for ref in (RP1, QP1, XP1, RP2, QP2, XP2, L0.Q):
        clear(ref)

    partners = [(lax.rem(gx + dx + NX, NX), lax.rem(gy + dy + NY, NY)) for dx, dy in SIDES]
    partners += [(gx, lax.rem(gy + k, NY)) for k in range(2, 7)]
    partners += [(lax.rem(gx + 2 * k, NX), gy) for k in range(1, 16)]
    barrier = pltpu.get_barrier_semaphore()
    for partner in partners:
        pl.semaphore_signal(barrier, inc=1, device_id=partner, device_id_type=MESH)

    values = jnp.zeros((8, 128), F32)
    for k in range(8):
        values = jnp.where(lane == k, table[k], values)
    for copy in loads:
        copy.wait()

    def look_up(i):
        for j, m in quad(0, 16):
            index = PH[i, pl.ds(j, m)]
            cells = pick_lane(jnp.broadcast_to(values, index.shape), index)
            L0.V[i + 3, pl.ds(j + 3, m)] = cells
            L0.R[i + 3, pl.ds(j + 3, m)] = choose(group == 3, cells, L0.R[i + 3, pl.ds(j + 3, m)])

    loop(0, 16, look_up)
    pl.semaphore_wait(barrier, len(partners))

    pending = halo_copies(L0.R, (16, 16), (3, 3), (2, 2), (2, 2), gx, gy, send, recv, 0, 8)
    for k, (dx, dy) in enumerate(((-1, 0), (1, 0), (0, -1), (0, 1))):
        span = {0: (pl.ds(3, 16), pl.ds(3, 16)), -1: (pl.ds(5, 1), pl.ds(21, 1)), 1: (pl.ds(16, 1), pl.ds(0, 1))}
        pending.append(
            pltpu.make_async_remote_copy(
                src_ref=L0.R.at[span[dx][0], span[dy][0], pl.ds(6, 2)],
                dst_ref=L0.R.at[span[dx][1], span[dy][1], pl.ds(6, 2)],
                send_sem=send.at[8 + k],
                recv_sem=recv.at[8 + k],
                device_id=(lax.rem(gx + dx + NX, NX), lax.rem(gy + dy + NY, NY)),
                device_id_type=MESH,
            )
        )
    for copy in pending:
        copy.start()
    faces = pending
    sent = []

    def restrict(src, halo_src, count, reach, i):
        row = src[halo_src + 2 * i, pl.ds(halo_src, count)] + src[halo_src + 2 * i + 1, pl.ds(halo_src, count)]
        row = row.reshape(count // 2, 2, 8, 128)
        return pair_sum(row[:, 0] + row[:, 1], reach) * 0.125

    def coarsen_v1(i):
        L1.V[4 + i, pl.ds(4, 8)] = restrict(L0.V, 3, 16, 1, i)

    def coarsen_v2(i):
        L2.V[4 + i, pl.ds(4, 4)] = restrict(L1.V, 4, 8, 2, i)

    loop(0, 8, coarsen_v1)
    loop(0, 4, coarsen_v2)

    def pack_v1(a):
        for b in range(2):
            parts = [by_group([L1.V[4 + 2 * a + p, 4 + 4 * b + k] for k in range(4)]) for p in range(2)]
            VP1[a + 2, b + 1] = jnp.where(lane % 2 == 0, parts[0], parts[1])

    loop(0, 4, pack_v1)
    tile = None
    for p in range(4):
        part = by_group([L2.V[4 + p, 4 + k] for k in range(4)])
        tile = part if tile is None else jnp.where(lane % 4 == p, part, tile)
    VP2[1, 1] = tile

    for copy in pending:
        copy.wait_recv()

    early = halo_copies(VP1, (4, 2), (2, 1), (2, 1), (2, 1), gx, gy, send, recv, 12, 8)
    early += halo_copies(VP2, (1, 1), (1, 1), (1, 1), (1, 1), gx, gy, send, recv, 20, 8)
    for copy in early:
        copy.start()
    sent += early

    def fill_v0(i):
        for j, m in quad(0, 22):
            L0.V[i, pl.ds(j, m)] = spread_sub(L0.R[i, pl.ds(j, m)], 3)

    loop(0, 22, fill_v0)
    L0.build(gx, gy, kinds, 1, 21)
    L0.descend()
    for copy in faces:
        copy.wait_send()

    def pack_r1(a):
        one, other = restrict(L0.Q, 3, 16, 1, 2 * a), restrict(L0.Q, 3, 16, 1, 2 * a + 1)
        RP1[a + 1, pl.ds(2, 8)] = choose(lane % 2 == 0, one, other)

    loop(0, 4, pack_r1)
    pending = halo_copies(RP1, (4, 8), (1, 2), (1, 2), (1, 1), gx, gy, send, recv, 28)
    for copy in pending:
        copy.start()
    sent += pending
    for copy in early:
        copy.wait_recv()

    def unpack_v1(a):
        for b in range(4):
            both = VP1[a, b]
            for p in range(2):
                part = pick_lane(both, (lane // 2) * 2 + p)
                for k in range(4):
                    L1.V[2 * a + p, 4 * b + k] = spread_sub(part, k)

    loop(0, 8, unpack_v1)

    def unpack_v2(a):
        for b in range(3):
            both = VP2[a, b]
            for p in range(4):
                part = pick_lane(both, (lane // 4) * 4 + p)
                for k in range(4):
                    L2.V[4 * a + p, 4 * b + k] = spread_sub(part, k)

    loop(0, 3, unpack_v2)
    L1.build(gx, gy, kinds, 1, 15)
    L2.build(gx, gy, kinds, 1, 11)
    for copy in pending:
        copy.wait_recv()

    def unpack_pairs(src, dst, count, x_first, y_first, y_count):
        def body(a):
            row = src[a, pl.ds(0, y_count)]
            for p in range(2):
                dst[x_first + 2 * a + p, pl.ds(y_first, y_count)] = pick_lane(row, (lane // 2) * 2 + p)

        loop(0, count, body)

    unpack_pairs(RP1, L1.R, 6, 2, 2, 12)
    L1.descend()

    def pack_r2(a):
        rows = []
        for p in range(2):
            row = restrict(L1.Q, 4, 8, 2, 2 * a + p).reshape(2, 2, 8, 128)
            rows.append(choose(lane % 2 == 0, row[:, 0], row[:, 1]))
        RP2[a + 1, pl.ds(1, 2)] = choose(lane % 4 < 2, rows[0], rows[1])

    loop(0, 2, pack_r2)
    pending = halo_copies(RP2, (2, 2), (1, 1), (1, 1), (1, 1), gx, gy, send, recv, 36)
    for copy in pending:
        copy.start()
    sent += pending
    late0 = halo_copies(L0.Q, (16, 16), (3, 3), (2, 2), (1, 1), gx, gy, send, recv, 99)
    for copy in late0:
        copy.start()
    sent += late0
    for copy in pending:
        copy.wait_recv()

    def unpack_quads(src, dst, count, first):
        def body(a):
            for b in range(count):
                both = src[a, b]
                for p in range(2):
                    for k in range(2):
                        dst[first + 2 * a + p, first + 2 * b + k] = pick_lane(both, (lane // 4) * 4 + (2 * p + k))

        loop(0, count, body)

    unpack_quads(RP2, L2.R, 4, 2)
    L2.descend()

    for p in range(2):
        r3 = restrict(L2.Q, 4, 4, 4, p)
        v3 = restrict(L2.V, 4, 4, 4, p)
        both = choose(group == 3, v3, r3)
        both = pick_lane(both, 8 * (lane % 16))
        both = jnp.where(tiled(lane // 16 == subs(), both), both, 0.0)
        for k in range(2):
            MSG[pl.ds(2 * p + k, 1), :] = jnp.sum(both[k], axis=0, keepdims=True)
    rows = pl.ds(pl.multiple_of(4 * gy, 4), 4)
    keep = pltpu.make_async_copy(MSG.at[pl.ds(0, 4)], CG.at[pair, core, rows], in_sem.at[0])
    keep.start()
    pending = []
    for k in range(1, 16):
        pending.append(
            pltpu.make_async_remote_copy(
                src_ref=MSG.at[pl.ds(0, 4)],
                dst_ref=CG.at[pair, core, rows],
                send_sem=send.at[44 + k - 1],
                recv_sem=recv.at[44 + k - 1],
                device_id=(lax.rem(gx + 2 * k, NX), gy),
                device_id_type=MESH,
            )
        )
    for copy in pending:
        copy.start()
    sent += pending

    def pack_1(a):
        for src, dst, x0, y0 in ((L1.Q, QP1, 2, 3), (L1.X, XP1, 1, 2)):
            one, other = src[4 + 2 * a, pl.ds(4, 8)], src[5 + 2 * a, pl.ds(4, 8)]
            dst[x0 + a, pl.ds(y0, 8)] = choose(lane % 2 == 0, one, other)

    loop(0, 4, pack_1)

    def pack_2(a):
        for src, dst, x0 in ((L2.Q, QP2, 2), (L2.X, XP2, 1)):
            mixed = []
            for p in range(2):
                row = src[4 + 2 * a + p, pl.ds(4, 4)].reshape(2, 2, 8, 128)
                mixed.append(choose(lane % 2 == 0, row[:, 0], row[:, 1]))
            dst[x0 + a, pl.ds(x0, 2)] = choose(lane % 4 < 2, mixed[0], mixed[1])

    loop(0, 2, pack_2)
    late2 = halo_copies(QP2, (2, 2), (2, 2), (2, 2), (2, 2), gx, gy, send, recv, 67)
    late2 += halo_copies(XP2, (2, 2), (1, 1), (1, 1), (1, 1), gx, gy, send, recv, 75)
    late1 = halo_copies(QP1, (4, 8), (2, 3), (2, 3), (1, 2), gx, gy, send, recv, 83)
    late1 += halo_copies(XP1, (4, 8), (1, 2), (1, 2), (1, 1), gx, gy, send, recv, 91)
    for copy in late2 + late1:
        copy.start()
    sent += late2 + late1
    keep.wait()
    for copy in pending:
        copy.wait_recv()

    pending = []
    for k in range(1, 8):
        pending.append(
            pltpu.make_async_remote_copy(
                src_ref=CG.at[:, core, rows],
                dst_ref=CG.at[:, core, rows],
                send_sem=send.at[59 + k - 1],
                recv_sem=recv.at[59 + k - 1],
                device_id=(gx, lax.rem(gy + k, NY)),
                device_id_type=MESH,
            )
        )
    for copy in pending:
        copy.start()
    sent += pending
    for copy in pending:
        copy.wait_recv()
    swap = pltpu.make_async_remote_copy(
        src_ref=CG.at[:, core],
        dst_ref=CG.at[:, core],
        send_sem=send.at[66],
        recv_sem=recv.at[66],
        device_id=(gx + 1 - 2 * core, gy),
        device_id_type=MESH,
    )
    swap.start()
    sent.append(swap)
    swap.wait_recv()

    coarse(gx, gy, kinds, CG, CR, CV, KXM, KXP, KA, KB, KZ, CD, CI, CS, CE)

    flat = CE.reshape(96, 128)

    def expand(a):
        for j in range(6):
            row = 16 * a + 8 * (j % 2) + lax.rem(gy + 7 + j // 2, 8)
            both = jnp.broadcast_to(flat[pl.ds(row, 1), :], (8, 128))
            both = pick_lane(both, 16 * subs() + lane // 8)
            for p in range(2):
                for k in range(2):
                    L2.PR[2 * a + p, 2 * j + k] = both

    loop(0, 6, expand)

    for copy in late2:
        copy.wait_recv()
    unpack_quads(QP2, L2.Q, 6, 0)
    unpack_quads(XP2, L2.X, 4, 2)

    def middle(level):
        h, b = level.halo, level.block
        level.correct(h - 3, h + b + 3)
        level.second_step(level.R, level.R, h - 2, h + b + 2)

        def body(i):
            for j, m in quad(h - 2, h + b + 2):
                here = pl.ds(j, m)
                level.SB[i, here] = (level.X[i, here] + level.PR[i, here]) + (level.SA[i, here] + level.SB[i, here])

        loop(h - 2, h + b + 2, body)

    middle(L2)
    L1.lift(L2.SB, (0, 2), 2, 8)
    for copy in late1:
        copy.wait_recv()

    def unpack_q1(a):
        row = QP1[a]
        for p in range(2):
            L1.Q[2 * a + p, pl.ds(1, 14)] = pick_lane(row, (lane // 2) * 2 + p)

    loop(0, 8, unpack_q1)
    unpack_pairs(XP1, L1.X, 6, 2, 2, 12)
    middle(L1)
    L0.lift(L1.SB, (1, 2), 2, 12)
    for copy in late0:
        copy.wait_recv()
    L0.correct(1, 21)
    L0.second_step(L0.R, L0.R, 2, 20)

    def last(i):
        for j, m in quad(3, 19):
            here = pl.ds(j, m)
            step, near = L0.near(L0.SB, i, j, m)
            diag = L0.D[i, here]
            field = (L0.X[i, here] + L0.PR[i, here]) + (L0.SA[i, here] + step)
            L0.R[i, here] = L0.R[i, here] - diag * step + near
            OW[i - 3, pl.ds(j - 3, m)] = diag * field

    loop(3, 19, last)
    stores = []
    for c in range(3):
        for s in range(2):
            place = pl.ds(128 * s, 128)
            stores.append(
                pltpu.make_async_copy(OW.at[:, :, 2 * c + s], out_w.at[c, :, :, place], in_sem.at[len(stores)])
            )
            stores.append(
                pltpu.make_async_copy(
                    L0.R.at[pl.ds(3, 16), pl.ds(3, 16), 2 * c + s],
                    out_r.at[c, :, :, place],
                    in_sem.at[len(stores)],
                )
            )
    for copy in stores:
        copy.start()
    for copy in sent:
        copy.wait_send()
    for copy in stores:
        copy.wait()


def coarse(gx, gy, kinds, CG, CR, CV, KXM, KXP, KA, KB, KZ, CD, CI, CS, CE):
    planes = 2 * NX
    scale = 0.25 ** (LEVELS - 1)
    lane = lanes()
    spot = lane % 32
    flat = CG.reshape(1024, 128)

    def blocks(reach, body):
        lo = jnp.maximum(2 * gx - 2 - reach, 0) // BLOCK
        hi = (jnp.minimum(2 * gx + 4 + reach, planes) + BLOCK - 1) // BLOCK
        loop(lo, hi, body)

    zeros = jnp.zeros((PAD, 2, 8, 128), F32)
    for place in (0, PAD + planes):
        CV[pl.ds(place, PAD)] = zeros
        CS[0, pl.ds(place, PAD)] = zeros
        CS[1, pl.ds(place, PAD)] = zeros

    def take(b):
        for q in range(BLOCK):
            for y in range(2):
                start = 16 * BLOCK * b + 32 * (q // 2) + 2 * (q % 2) + y
                row = flat[pl.ds(start, 8, stride=4), :]
                CR[PAD + BLOCK * b + q, y] = row
                CV[PAD + BLOCK * b + q, y] = pick_lane(row, 96 + spot)

    blocks(26, take)

    def per_kind(wall):
        tile = jnp.zeros((8, 128), F32)
        for c in range(3):
            tile = jnp.where(lane // 32 == c, kinds[c, wall].astype(F32), tile)
        return tile

    walls = [per_kind(wall) for wall in range(6)]
    z_wall = jnp.where(spot == 0, walls[4], 0.0) + jnp.where(spot == 31, walls[5], 0.0)
    low_y = z_wall + jnp.where(subs() == 0, walls[2], 0.0)
    high_y = z_wall + jnp.where(subs() == 7, walls[3], 0.0)

    def setup(b):
        here = pl.ds(PAD + BLOCK * b, BLOCK)
        prev, after = pl.ds(PAD - 1 + BLOCK * b, BLOCK), pl.ds(PAD + 1 + BLOCK * b, BLOCK)
        plane = lax.broadcasted_iota(jnp.int32, (BLOCK, 8, 128), 0) + BLOCK * b
        even, odd = CV[here, 0], CV[here, 1]
        half = 0.5 * scale
        ka = half * (even + odd)
        kb = half * (odd + roll_sub(even, -1))
        kb = jnp.where(tiled(subs() == 7, kb), 0.0, kb)
        KA[here] = ka
        KB[here] = kb
        x_wall = jnp.where(plane == 0, tiled(walls[0], even), 0.0)
        x_wall = x_wall + jnp.where(plane == planes - 1, tiled(walls[1], even), 0.0)
        for y, value, wall, other in ((0, even, low_y, roll_sub(kb, 1)), (1, odd, high_y, kb)):
            kxm = jnp.where(plane == 0, 0.0, half * (CV[prev, y] + value))
            kxp = jnp.where(plane == planes - 1, 0.0, half * (value + CV[after, y]))
            kz = half * (value + roll_lane(value, -1))
            kz = jnp.where(tiled(spot == 31, kz), 0.0, kz)
            KXM[here, y] = kxm
            KXP[here, y] = kxp
            KZ[here, y] = kz
            total = (kxm + kxp) + (ka + other) + (kz + roll_lane(kz, 1))
            total = total + (2.0 * scale) * value * (x_wall + tiled(wall, value))
            CD[here, y] = total
            inverse = 1.0 / total
            CI[here, y] = inverse
            CS[0, here, y] = CR[here, y] * inverse * (1.0 / CMID)

    blocks(25, setup)

    own = pl.ds(PAD - 2 + 2 * gx, 6)
    CE[...] = CS[0, own]

    def sweep(k, rho):
        now, later = lax.rem(k, 2), lax.rem(k + 1, 2)
        rho_next = 1.0 / (2.0 * CSIG - rho)
        step_a = rho_next * rho
        step_b = rho_next * (2.0 / CRAD)

        def body(b):
            here = pl.ds(PAD + BLOCK * b, BLOCK)
            prev, after = pl.ds(PAD - 1 + BLOCK * b, BLOCK), pl.ds(PAD + 1 + BLOCK * b, BLOCK)
            even, odd = CS[now, here, 0], CS[now, here, 1]
            ka, kb = KA[here], KB[here]
            for y, value, beside in (
                (0, even, ka * odd + roll_sub(kb * odd, 1)),
                (1, odd, ka * even + kb * roll_sub(even, -1)),
            ):
                kz = KZ[here, y]
                near = KXM[here, y] * CS[now, prev, y] + KXP[here, y] * CS[now, after, y] + beside
                near = near + (kz * roll_lane(value, -1) + roll_lane(kz * value, 1))
                r = CR[here, y] - CD[here, y] * value + near
                CR[here, y] = r
                CS[later, here, y] = tiled(step_a, r) * value + tiled(step_b, r) * (r * CI[here, y])

        blocks(CSWEEPS - 2 - k, body)
        CE[...] = CE[...] + CS[later, own]
        return rho_next

    lax.fori_loop(0, CSWEEPS - 1, sweep, jnp.full((8, 128), 1.0 / CSIG, F32))


def per_device(body_force, phase, viscosity_table, wall_kinds):
    def vmem(*lead):
        return pltpu.VMEM(lead + (8, 128), F32)

    scratch = [
        pltpu.VMEM((16, 16, 8, 128), jnp.int32),
        vmem(6, 12), vmem(8, 4), vmem(8, 14), vmem(6, 12),
        vmem(4, 4), vmem(3, 3), vmem(6, 6), vmem(4, 4),
        vmem(), pltpu.VMEM((16, 2, 32, 128), F32),
    ]
    depth = 2 * NX + 2 * PAD
    scratch += [vmem(depth, 2)] * 4 + [vmem(depth)] * 2 + [vmem(depth, 2)] * 3 + [vmem(2, depth, 2), vmem(6, 2)]
    scratch += [vmem(16, 16)]
    for frame in (22, 16, 12):
        scratch += [vmem(frame, frame)] * 12
    n_sems = 107
    scratch += [pltpu.SemaphoreType.DMA((14,)), pltpu.SemaphoreType.DMA((n_sems,)), pltpu.SemaphoreType.DMA((n_sems,))]
    shape = jax.ShapeDtypeStruct(body_force.shape, F32)
    return pl.pallas_call(
        kernel,
        out_shape=(shape, shape),
        in_specs=[
            pl.BlockSpec(memory_space=pl.ANY),
            pl.BlockSpec(memory_space=pl.ANY),
            pl.BlockSpec(memory_space=pltpu.SMEM),
            pl.BlockSpec(memory_space=pltpu.SMEM),
        ],
        out_specs=(pl.BlockSpec(memory_space=pl.ANY), pl.BlockSpec(memory_space=pl.ANY)),
        scratch_shapes=scratch,
        compiler_params=pltpu.CompilerParams(
            collective_id=0, has_side_effects=True, vmem_limit_bytes=56 * 2**20
        ),
        name="vcycle",
    )(body_force, phase, viscosity_table, wall_kinds)


def solution(mesh):
    placed = (P(None, "gx", "gy", None), P("gx", "gy", None), P(), P())
    return jax.shard_map(
        per_device,
        mesh=mesh,
        in_specs=placed,
        out_specs=(P(None, "gx", "gy", None), P(None, "gx", "gy", None)),
        check_vma=False,
    )
```

```python
import jax
import jax.numpy as jnp
from jax import lax
from jax.experimental import pallas as pl
from jax.experimental.pallas import tpu as pltpu
from jax.sharding import PartitionSpec as P


F32 = jnp.float32
MESH = pl.DeviceIdType.MESH
LEVELS = 4
CSWEEPS = 24
NX = 32
NY = 8
LOW, HIGH = 0.2, 2.0
CLOW, CHIGH = 0.05, 2.0

MID = (HIGH + LOW) / 2.0
RAD = (HIGH - LOW) / 2.0
SIG = MID / RAD
RHO0 = 1.0 / SIG
RHO1 = 1.0 / (2.0 * SIG - RHO0)
STEP_A = RHO1 * RHO0
STEP_B = 2.0 * RHO1 / RAD

CMID = (CHIGH + CLOW) / 2.0
CRAD = (CHIGH - CLOW) / 2.0
CSIG = CMID / CRAD

SIDES = [(dx, dy) for dx in (-1, 0, 1) for dy in (-1, 0, 1) if dx or dy]
PAD = 4
BLOCK = 16
PLANES = 8
CHUNK = 8


def lanes():
    return lax.broadcasted_iota(jnp.int32, (8, 128), 1)


def subs():
    return lax.broadcasted_iota(jnp.int32, (8, 128), 0)


def tiled(index, values):
    return jnp.broadcast_to(index, values.shape)


def roll_lane(values, shift):
    return pltpu.roll(values, shift % 128, values.ndim - 1)


def roll_sub(values, shift):
    return pltpu.roll(values, shift % 8, values.ndim - 2)


def pick_lane(values, index):
    return jnp.take_along_axis(values, tiled(index, values), axis=values.ndim - 1, mode="promise_in_bounds")


def choose(mask, one, other):
    return jnp.where(tiled(mask, one), one, other)


def above(values, reach):
    moved = roll_lane(values, -reach)
    return choose(lanes() >= 128 - reach, roll_sub(moved, -1), moved)


def below(values, reach):
    moved = roll_lane(values, reach)
    return choose(lanes() < reach, roll_sub(moved, 1), moved)


def pair_sum(values, reach):
    return values + choose((lanes() & reach) == 0, roll_lane(values, -reach), roll_lane(values, reach))


def spread_sub(values, group):
    kept = jnp.where(tiled(subs() // 2 == group, values), values, 0.0)
    kept = kept + roll_sub(kept, 2)
    return kept + roll_sub(kept, 4)


def by_group(parts):
    group = subs() // 2
    out = parts[3]
    for k in (2, 1, 0):
        out = choose(group == k, parts[k], out)
    return out


def quad(lo, hi):
    return [(j, min(CHUNK, hi - j)) for j in range(lo, hi, CHUNK)]


def loop(lo, hi, body, width=CHUNK):
    whole = isinstance(lo, int) and isinstance(hi, int)
    most = 7 if width <= 4 else 4
    turns = next(k for k in range(most, 0, -1) if k == 1 or whole and (hi - lo) % k == 0)

    def step(t, carry):
        for k in range(turns):
            body(lo + turns * t + k)
        return carry

    lax.fori_loop(0, (hi - lo) // turns, step, 0)


def clear(ref):
    rows, columns = ref.shape[:2]

    def body(i):
        ref[i] = jnp.zeros((columns, 8, 128), F32)

    loop(0, rows, body)


class Level:
    def __init__(self, index, block, halo, refs):
        self.block, self.halo = block, halo
        self.frame = block + 2 * halo
        self.reach = 2**index
        self.scale = 0.25**index
        self.V, self.KX, self.KY, self.KZ, self.D, self.I, self.R, self.SA, self.SB, self.Q, self.X, self.PR = refs

    def near(self, ref, i, j, m):
        wide = ref[i, pl.ds(j - 1, m + 2)]
        mid = wide[1:-1]
        ky = self.KY[i, pl.ds(j, m + 1)]
        kz = self.KZ[i, pl.ds(j, m)]
        out = self.KX[i, pl.ds(j, m)] * ref[i - 1, pl.ds(j, m)]
        out = out + self.KX[i + 1, pl.ds(j, m)] * ref[i + 1, pl.ds(j, m)]
        out = out + (ky[:-1] * wide[:-2] + ky[1:] * wide[2:])
        out = out + (kz * above(mid, self.reach) + below(kz * mid, self.reach))
        return mid, out

    def build(self, gx, gy, kinds, top, bottom, lo, hi):
        h, b = self.halo, self.block
        half = 0.5 * self.scale
        group, side = subs() // 2, subs() % 2

        def per_kind(wall):
            tile = jnp.zeros((8, 128), F32)
            for c in range(3):
                tile = jnp.where(group == c, kinds[c, wall].astype(F32), tile)
            return tile

        walls = [per_kind(wall) for wall in range(6)]
        z_low = (side == 0) & (lanes() < self.reach)
        z_high = (side == 1) & (lanes() >= 128 - self.reach)
        z_wall = jnp.where(z_low, walls[4], 0.0) + jnp.where(z_high, walls[5], 0.0)
        one, zero = jnp.float32(1.0), jnp.float32(0.0)
        at_x = (jnp.where(gx == 0, one, zero), jnp.where(gx == NX - 1, one, zero))
        at_y = (jnp.where(gy == 0, one, zero), jnp.where(gy == NY - 1, one, zero))

        def faces(i):
            place = gx * b + i - h
            open_x = jnp.where((place == 0) | (place == NX * b), zero, one)
            for j, m in quad(lo, hi):
                here = self.V[i, pl.ds(j, m)]
                self.KX[i, pl.ds(j, m)] = (half * open_x) * (self.V[i - 1, pl.ds(j, m)] + here)

        loop(top, bottom + 1, faces, hi - lo)

        def rest(i):
            x_wall = z_wall + jnp.where(i == h, at_x[0], zero) * walls[0]
            x_wall = x_wall + jnp.where(i == h + b - 1, at_x[1], zero) * walls[1]
            for j, m in quad(lo, hi + 1):
                self.KY[i, pl.ds(j, m)] = half * (self.V[i, pl.ds(j - 1, m)] + self.V[i, pl.ds(j, m)])
            for j, at in ((h, at_y[0]), (h + b, at_y[1])):
                if lo <= j <= hi:
                    self.KY[i, j] = self.KY[i, j] * (one - at)
            for j, m in quad(lo, hi):
                here = self.V[i, pl.ds(j, m)]
                ky = self.KY[i, pl.ds(j, m + 1)]
                kz = half * (here + above(here, self.reach))
                kz = jnp.where(tiled(z_high, kz), 0.0, kz)
                self.KZ[i, pl.ds(j, m)] = kz
                total = self.KX[i, pl.ds(j, m)] + self.KX[i + 1, pl.ds(j, m)] + (ky[:-1] + ky[1:])
                total = total + (kz + below(kz, self.reach))
                self.D[i, pl.ds(j, m)] = total + (2.0 * self.scale) * here * tiled(x_wall, here)
            for j, wall, at in ((h, walls[2], at_y[0]), (h + b - 1, walls[3], at_y[1])):
                if lo <= j < hi:
                    self.D[i, j] = self.D[i, j] + (2.0 * self.scale * at) * self.V[i, j] * wall
            for j, m in quad(lo, hi):
                self.I[i, pl.ds(j, m)] = 1.0 / self.D[i, pl.ds(j, m)]

        loop(top, bottom, rest, hi - lo)

    def first_step(self, src, top, bottom, lo, hi):
        def body(i):
            for j, m in quad(lo, hi):
                self.SA[i, pl.ds(j, m)] = src[i, pl.ds(j, m)] * self.I[i, pl.ds(j, m)] * (1.0 / MID)

        loop(top, bottom, body, hi - lo)

    def second_step(self, src, dst, top, bottom, lo, hi):
        def body(i):
            for j, m in quad(lo, hi):
                step, near = self.near(self.SA, i, j, m)
                r = src[i, pl.ds(j, m)] * (1.0 - 1.0 / MID) + near
                dst[i, pl.ds(j, m)] = r
                self.SB[i, pl.ds(j, m)] = STEP_A * step + STEP_B * (r * self.I[i, pl.ds(j, m)])

        loop(top, bottom, body, hi - lo)

    def third_step(self, top, bottom, lo, hi):
        def body(i):
            for j, m in quad(lo, hi):
                step, near = self.near(self.SB, i, j, m)
                self.Q[i, pl.ds(j, m)] = self.Q[i, pl.ds(j, m)] - self.D[i, pl.ds(j, m)] * step + near
                self.X[i, pl.ds(j, m)] = self.SA[i, pl.ds(j, m)] + step

        loop(top, bottom, body, hi - lo)

    def descend(self, parts=None):
        h, e = self.halo, self.halo + self.block
        parts = parts or (lambda lo, hi, margin: [(lo, hi, lo, hi)])
        for part in parts(h - 2, e + 2, 1):
            self.first_step(self.R, *part)
        for part in parts(h - 1, e + 1, 2):
            self.second_step(self.R, self.Q, *part)
        for part in parts(h, e, 3):
            self.third_step(*part)

    def lift(self, ref, shift, first, count):
        def body(i):
            row = ref[(i + shift[0]) // 2 + shift[1], pl.ds(first, count)]
            row = jnp.broadcast_to(row[:, None], (count, 2, 8, 128)).reshape(2 * count, 8, 128)
            skip = (2 * count - self.frame) // 2
            self.PR[i] = row[skip : skip + self.frame]

        loop(0, self.frame, body)

    def correct(self, lo, hi):
        def body(i):
            for j, m in quad(lo, hi):
                lifted, near = self.near(self.PR, i, j, m)
                q = self.Q[i, pl.ds(j, m)] - self.D[i, pl.ds(j, m)] * lifted + near
                self.R[i, pl.ds(j, m)] = q
                self.SA[i, pl.ds(j, m)] = q * self.I[i, pl.ds(j, m)] * (1.0 / MID)

        loop(lo, hi, body)


def halo_copies(ref, own, halo, cut, corner, gx, gy, send, recv, first, height=6):
    copies = []
    for k, (dx, dy) in enumerate(SIDES):
        src, dst = [], []
        wide = corner if dx and dy else cut
        for d, o, h, w in ((dx, own[0], halo[0], wide[0]), (dy, own[1], halo[1], wide[1])):
            if d == 0:
                src.append(pl.ds(h, o))
                dst.append(pl.ds(h, o))
            elif d < 0:
                src.append(pl.ds(h, w))
                dst.append(pl.ds(h + o, w))
            else:
                src.append(pl.ds(h + o - w, w))
                dst.append(pl.ds(h - w, w))
        target = (lax.rem(gx + dx + NX, NX), lax.rem(gy + dy + NY, NY))
        copies.append(
            pltpu.make_async_remote_copy(
                src_ref=ref.at[src[0], src[1], pl.ds(0, height)],
                dst_ref=ref.at[dst[0], dst[1], pl.ds(0, height)],
                send_sem=send.at[first + k],
                recv_sem=recv.at[first + k],
                device_id=target,
                device_id_type=MESH,
            )
        )
    return copies


def kernel(
    force, phase, table, kinds, out_w, out_r,
    PH, RP1, VP1, QP1, XP1, RP2, VP2, QP2, XP2, MSG, CG, CR, CV, KXM, KXP, KA, KB, KZ, CD, CI, CSA, CSB, CRB, CE, OW, *rest,
):
    refs0, refs1, refs2 = rest[0:12], rest[12:24], rest[24:36]
    in_sem, send, recv = rest[36:]
    gx, gy = lax.axis_index("gx"), lax.axis_index("gy")
    core = lax.rem(gx, 2)
    pair = gx // 2
    L0, L1, L2 = Level(0, 16, 3, refs0), Level(1, 8, 4, refs1), Level(2, 4, 4, refs2)
    group, side, lane = subs() // 2, subs() % 2, lanes()

    loads = []
    for c in range(3):
        for s in range(2):
            loads.append(
                pltpu.make_async_copy(
                    force.at[c, :, :, pl.ds(128 * s, 128)],
                    L0.R.at[pl.ds(3, 16), pl.ds(3, 16), 2 * c + s],
                    in_sem.at[len(loads)],
                )
            )
    for c in range(4):
        for s in range(2):
            loads.append(
                pltpu.make_async_copy(
                    phase.at[:, :, pl.ds(128 * s, 128)], PH.at[:, :, 2 * c + s], in_sem.at[len(loads)]
                )
            )
    for copy in loads:
        copy.start()

    for ref in (RP1, QP1, XP1, RP2, QP2, XP2, L0.Q):
        clear(ref)

    partners = [(lax.rem(gx + dx + NX, NX), lax.rem(gy + dy + NY, NY)) for dx, dy in SIDES]
    partners += [(gx, lax.rem(gy + k, NY)) for k in range(2, 7)]
    partners += [(lax.rem(gx + 2 * k, NX), gy) for k in range(1, 16)]
    barrier = pltpu.get_barrier_semaphore()
    for partner in partners:
        pl.semaphore_signal(barrier, inc=1, device_id=partner, device_id_type=MESH)

    values = jnp.zeros((8, 128), F32)
    for k in range(8):
        values = jnp.where(lane == k, table[k], values)
    for copy in loads:
        copy.wait()

    def look_up(i):
        for j, m in quad(0, 16):
            index = PH[i, pl.ds(j, m)]
            cells = pick_lane(jnp.broadcast_to(values, index.shape), index)
            L0.V[i + 3, pl.ds(j + 3, m)] = cells
            L0.R[i + 3, pl.ds(j + 3, m)] = choose(group == 3, cells, L0.R[i + 3, pl.ds(j + 3, m)])

    loop(0, 16, look_up)
    pl.semaphore_wait(barrier, len(partners))

    pending = halo_copies(L0.R, (16, 16), (3, 3), (2, 2), (2, 2), gx, gy, send, recv, 0, 8)
    for k, (dx, dy) in enumerate(((-1, 0), (1, 0), (0, -1), (0, 1))):
        span = {0: (pl.ds(3, 16), pl.ds(3, 16)), -1: (pl.ds(5, 1), pl.ds(21, 1)), 1: (pl.ds(16, 1), pl.ds(0, 1))}
        pending.append(
            pltpu.make_async_remote_copy(
                src_ref=L0.R.at[span[dx][0], span[dy][0], pl.ds(6, 2)],
                dst_ref=L0.R.at[span[dx][1], span[dy][1], pl.ds(6, 2)],
                send_sem=send.at[8 + k],
                recv_sem=recv.at[8 + k],
                device_id=(lax.rem(gx + dx + NX, NX), lax.rem(gy + dy + NY, NY)),
                device_id_type=MESH,
            )
        )
    for copy in pending:
        copy.start()
    faces = pending
    sent = []

    def restrict(src, halo_src, count, reach, i):
        row = src[halo_src + 2 * i, pl.ds(halo_src, count)] + src[halo_src + 2 * i + 1, pl.ds(halo_src, count)]
        row = row.reshape(count // 2, 2, 8, 128)
        return pair_sum(row[:, 0] + row[:, 1], reach) * 0.125

    def coarsen_v1(i):
        L1.V[4 + i, pl.ds(4, 8)] = restrict(L0.V, 3, 16, 1, i)

    def coarsen_v2(i):
        L2.V[4 + i, pl.ds(4, 4)] = restrict(L1.V, 4, 8, 2, i)

    loop(0, 8, coarsen_v1)
    loop(0, 4, coarsen_v2)

    def pack_v1(a):
        for b in range(2):
            parts = [by_group([L1.V[4 + 2 * a + p, 4 + 4 * b + k] for k in range(4)]) for p in range(2)]
            VP1[a + 2, b + 1] = jnp.where(lane % 2 == 0, parts[0], parts[1])

    loop(0, 4, pack_v1)
    tile = None
    for p in range(4):
        part = by_group([L2.V[4 + p, 4 + k] for k in range(4)])
        tile = part if tile is None else jnp.where(lane % 4 == p, part, tile)
    VP2[1, 1] = tile

    def inside(lo, hi, margin):
        return [(3 + margin, 19 - margin, 3 + margin, 19 - margin)]

    def around(lo, hi, margin):
        a, b = 3 + margin, 19 - margin
        return [(lo, a, lo, hi), (b, hi, lo, hi), (a, b, lo, a), (a, b, b, hi)]

    for part in inside(1, 21, 1):
        L0.build(gx, gy, kinds, *part)
    L0.descend(inside)
    for copy in pending:
        copy.wait_recv()

    early = halo_copies(VP1, (4, 2), (2, 1), (2, 1), (2, 1), gx, gy, send, recv, 12, 8)
    early += halo_copies(VP2, (1, 1), (1, 1), (1, 1), (1, 1), gx, gy, send, recv, 20, 8)
    for copy in early:
        copy.start()
    sent += early

    for top, bottom, lo, hi in around(0, 22, 0):

        def fill_v0(i):
            for j, m in quad(lo, hi):
                L0.V[i, pl.ds(j, m)] = spread_sub(L0.R[i, pl.ds(j, m)], 3)

        loop(top, bottom, fill_v0, hi - lo)
    for part in around(1, 21, 1):
        L0.build(gx, gy, kinds, *part)
    L0.descend(around)
    for copy in faces:
        copy.wait_send()

    def pack_r1(a):
        one, other = restrict(L0.Q, 3, 16, 1, 2 * a), restrict(L0.Q, 3, 16, 1, 2 * a + 1)
        RP1[a + 1, pl.ds(2, 8)] = choose(lane % 2 == 0, one, other)

    loop(0, 4, pack_r1)
    pending = halo_copies(RP1, (4, 8), (1, 2), (1, 2), (1, 1), gx, gy, send, recv, 28)
    for copy in pending:
        copy.start()
    sent += pending
    for copy in early:
        copy.wait_recv()

    def unpack_v1(a):
        for b in range(4):
            both = VP1[a, b]
            for p in range(2):
                part = pick_lane(both, (lane // 2) * 2 + p)
                for k in range(4):
                    L1.V[2 * a + p, 4 * b + k] = spread_sub(part, k)

    loop(0, 8, unpack_v1)

    def unpack_v2(a):
        for b in range(3):
            both = VP2[a, b]
            for p in range(4):
                part = pick_lane(both, (lane // 4) * 4 + p)
                for k in range(4):
                    L2.V[4 * a + p, 4 * b + k] = spread_sub(part, k)

    loop(0, 3, unpack_v2)
    L1.build(gx, gy, kinds, 1, 15, 1, 15)
    L2.build(gx, gy, kinds, 1, 11, 1, 11)
    for copy in pending:
        copy.wait_recv()

    def unpack_pairs(src, dst, count, x_first, y_first, y_count):
        def body(a):
            row = src[a, pl.ds(0, y_count)]
            for p in range(2):
                dst[x_first + 2 * a + p, pl.ds(y_first, y_count)] = pick_lane(row, (lane // 2) * 2 + p)

        loop(0, count, body)

    unpack_pairs(RP1, L1.R, 6, 2, 2, 12)
    L1.descend()

    def pack_r2(a):
        rows = []
        for p in range(2):
            row = restrict(L1.Q, 4, 8, 2, 2 * a + p).reshape(2, 2, 8, 128)
            rows.append(choose(lane % 2 == 0, row[:, 0], row[:, 1]))
        RP2[a + 1, pl.ds(1, 2)] = choose(lane % 4 < 2, rows[0], rows[1])

    loop(0, 2, pack_r2)
    pending = halo_copies(RP2, (2, 2), (1, 1), (1, 1), (1, 1), gx, gy, send, recv, 36)
    for copy in pending:
        copy.start()
    sent += pending
    late0 = halo_copies(L0.Q, (16, 16), (3, 3), (2, 2), (1, 1), gx, gy, send, recv, 99)
    for copy in late0:
        copy.start()
    sent += late0
    for copy in pending:
        copy.wait_recv()

    def unpack_quads(src, dst, count, first):
        def body(a):
            for b in range(count):
                both = src[a, b]
                for p in range(2):
                    for k in range(2):
                        dst[first + 2 * a + p, first + 2 * b + k] = pick_lane(both, (lane // 4) * 4 + (2 * p + k))

        loop(0, count, body)

    unpack_quads(RP2, L2.R, 4, 2)
    L2.descend()

    for p in range(2):
        r3 = restrict(L2.Q, 4, 4, 4, p)
        v3 = restrict(L2.V, 4, 4, 4, p)
        both = choose(group == 3, v3, r3)
        both = pick_lane(both, 8 * (lane % 16))
        both = jnp.where(tiled(lane // 16 == subs(), both), both, 0.0)
        for k in range(2):
            MSG[pl.ds(2 * p + k, 1), :] = jnp.sum(both[k], axis=0, keepdims=True)
    rows = pl.ds(pl.multiple_of(4 * gy, 4), 4)
    keep = pltpu.make_async_copy(MSG.at[pl.ds(0, 4)], CG.at[pair, core, rows], in_sem.at[0])
    keep.start()
    pending = []
    for k in range(1, 16):
        pending.append(
            pltpu.make_async_remote_copy(
                src_ref=MSG.at[pl.ds(0, 4)],
                dst_ref=CG.at[pair, core, rows],
                send_sem=send.at[44 + k - 1],
                recv_sem=recv.at[44 + k - 1],
                device_id=(lax.rem(gx + 2 * k, NX), gy),
                device_id_type=MESH,
            )
        )
    for copy in pending:
        copy.start()
    sent += pending

    def pack_1(a):
        for src, dst, x0, y0 in ((L1.Q, QP1, 2, 3), (L1.X, XP1, 1, 2)):
            one, other = src[4 + 2 * a, pl.ds(4, 8)], src[5 + 2 * a, pl.ds(4, 8)]
            dst[x0 + a, pl.ds(y0, 8)] = choose(lane % 2 == 0, one, other)

    loop(0, 4, pack_1)

    def pack_2(a):
        for src, dst, x0 in ((L2.Q, QP2, 2), (L2.X, XP2, 1)):
            mixed = []
            for p in range(2):
                row = src[4 + 2 * a + p, pl.ds(4, 4)].reshape(2, 2, 8, 128)
                mixed.append(choose(lane % 2 == 0, row[:, 0], row[:, 1]))
            dst[x0 + a, pl.ds(x0, 2)] = choose(lane % 4 < 2, mixed[0], mixed[1])

    loop(0, 2, pack_2)
    late2 = halo_copies(QP2, (2, 2), (2, 2), (2, 2), (2, 2), gx, gy, send, recv, 67)
    late2 += halo_copies(XP2, (2, 2), (1, 1), (1, 1), (1, 1), gx, gy, send, recv, 75)
    late1 = halo_copies(QP1, (4, 8), (2, 3), (2, 3), (1, 2), gx, gy, send, recv, 83)
    late1 += halo_copies(XP1, (4, 8), (1, 2), (1, 2), (1, 1), gx, gy, send, recv, 91)
    keep.wait()
    for copy in pending:
        copy.wait_recv()

    pending = []
    for k in range(1, 8):
        pending.append(
            pltpu.make_async_remote_copy(
                src_ref=CG.at[:, core, rows],
                dst_ref=CG.at[:, core, rows],
                send_sem=send.at[59 + k - 1],
                recv_sem=recv.at[59 + k - 1],
                device_id=(gx, lax.rem(gy + k, NY)),
                device_id_type=MESH,
            )
        )
    for copy in pending:
        copy.start()
    sent += pending
    for copy in pending:
        copy.wait_recv()
    swap = pltpu.make_async_remote_copy(
        src_ref=CG.at[:, core],
        dst_ref=CG.at[:, core],
        send_sem=send.at[66],
        recv_sem=recv.at[66],
        device_id=(gx + 1 - 2 * core, gy),
        device_id_type=MESH,
    )
    swap.start()
    sent.append(swap)
    for copy in late2 + late1:
        copy.start()
    sent += late2 + late1
    swap.wait_recv()

    coarse(gx, gy, kinds, CG, CR, CV, KXM, KXP, KA, KB, KZ, CD, CI, CSA, CSB, CRB, CE)

    flat = CE.reshape(96, 128)

    def expand(a):
        for j in range(6):
            row = 16 * a + 8 * (j % 2) + lax.rem(gy + 7 + j // 2, 8)
            both = jnp.broadcast_to(flat[pl.ds(row, 1), :], (8, 128))
            both = pick_lane(both, 16 * subs() + lane // 8)
            for p in range(2):
                for k in range(2):
                    L2.PR[2 * a + p, 2 * j + k] = both

    loop(0, 6, expand)

    for copy in late2:
        copy.wait_recv()
    unpack_quads(QP2, L2.Q, 6, 0)
    unpack_quads(XP2, L2.X, 4, 2)

    def middle(level):
        h, b = level.halo, level.block
        level.correct(h - 3, h + b + 3)
        level.second_step(level.R, level.R, h - 2, h + b + 2, h - 2, h + b + 2)

        def body(i):
            for j, m in quad(h - 2, h + b + 2):
                here = pl.ds(j, m)
                level.SB[i, here] = (level.X[i, here] + level.PR[i, here]) + (level.SA[i, here] + level.SB[i, here])

        loop(h - 2, h + b + 2, body)

    middle(L2)
    L1.lift(L2.SB, (0, 2), 2, 8)
    for copy in late1:
        copy.wait_recv()

    def unpack_q1(a):
        row = QP1[a]
        for p in range(2):
            L1.Q[2 * a + p, pl.ds(1, 14)] = pick_lane(row, (lane // 2) * 2 + p)

    loop(0, 8, unpack_q1)
    unpack_pairs(XP1, L1.X, 6, 2, 2, 12)
    middle(L1)
    L0.lift(L1.SB, (1, 2), 2, 12)
    for copy in late0:
        copy.wait_recv()
    L0.correct(1, 21)
    L0.second_step(L0.R, L0.R, 2, 20, 2, 20)

    def last(i):
        for j, m in quad(3, 19):
            here = pl.ds(j, m)
            step, near = L0.near(L0.SB, i, j, m)
            diag = L0.D[i, here]
            field = (L0.X[i, here] + L0.PR[i, here]) + (L0.SA[i, here] + step)
            L0.R[i, here] = L0.R[i, here] - diag * step + near
            OW[i - 3, pl.ds(j - 3, m)] = diag * field

    loop(3, 19, last)
    stores = []
    for c in range(3):
        for s in range(2):
            place = pl.ds(128 * s, 128)
            stores.append(
                pltpu.make_async_copy(OW.at[:, :, 2 * c + s], out_w.at[c, :, :, place], in_sem.at[len(stores)])
            )
            stores.append(
                pltpu.make_async_copy(
                    L0.R.at[pl.ds(3, 16), pl.ds(3, 16), 2 * c + s],
                    out_r.at[c, :, :, place],
                    in_sem.at[len(stores)],
                )
            )
    for copy in stores:
        copy.start()
    for copy in sent:
        copy.wait_send()
    for copy in stores:
        copy.wait()


def coarse(gx, gy, kinds, CG, CR, CV, KXM, KXP, KA, KB, KZ, CD, CI, CSA, CSB, CRB, CE):
    planes = 2 * NX
    scale = 0.25 ** (LEVELS - 1)
    lane = lanes()
    spot = lane % 32
    flat = CG.reshape(1024, 128)

    def blocks(reach, body):
        lo = jnp.maximum(2 * gx - 2 - reach, 0) // BLOCK
        hi = (jnp.minimum(2 * gx + 4 + reach, planes) + BLOCK - 1) // BLOCK
        loop(lo, hi, body)

    zeros = jnp.zeros((PAD, 2, 8, 128), F32)
    for place in (0, PAD + planes):
        CV[pl.ds(place, PAD)] = zeros
        CSA[pl.ds(place, PAD)] = zeros
        CSB[pl.ds(place, PAD)] = zeros

    def take(b):
        for q in range(BLOCK):
            for y in range(2):
                start = 16 * BLOCK * b + 32 * (q // 2) + 2 * (q % 2) + y
                row = flat[pl.ds(start, 8, stride=4), :]
                CR[PAD + BLOCK * b + q, y] = row
                CV[PAD + BLOCK * b + q, y] = pick_lane(row, 96 + spot)

    blocks(26, take)

    def per_kind(wall):
        tile = jnp.zeros((8, 128), F32)
        for c in range(3):
            tile = jnp.where(lane // 32 == c, kinds[c, wall].astype(F32), tile)
        return tile

    walls = [per_kind(wall) for wall in range(6)]
    z_wall = jnp.where(spot == 0, walls[4], 0.0) + jnp.where(spot == 31, walls[5], 0.0)
    low_y = z_wall + jnp.where(subs() == 0, walls[2], 0.0)
    high_y = z_wall + jnp.where(subs() == 7, walls[3], 0.0)

    def setup(b):
        here = pl.ds(PAD + BLOCK * b, BLOCK)
        prev, after = pl.ds(PAD - 1 + BLOCK * b, BLOCK), pl.ds(PAD + 1 + BLOCK * b, BLOCK)
        plane = lax.broadcasted_iota(jnp.int32, (BLOCK, 8, 128), 0) + BLOCK * b
        even, odd = CV[here, 0], CV[here, 1]
        half = 0.5 * scale
        ka = half * (even + odd)
        kb = half * (odd + roll_sub(even, -1))
        kb = jnp.where(tiled(subs() == 7, kb), 0.0, kb)
        KA[here] = ka
        KB[here] = kb
        x_wall = jnp.where(plane == 0, tiled(walls[0], even), 0.0)
        x_wall = x_wall + jnp.where(plane == planes - 1, tiled(walls[1], even), 0.0)
        for y, value, wall, other in ((0, even, low_y, roll_sub(kb, 1)), (1, odd, high_y, kb)):
            kxm = jnp.where(plane == 0, 0.0, half * (CV[prev, y] + value))
            kxp = jnp.where(plane == planes - 1, 0.0, half * (value + CV[after, y]))
            kz = half * (value + roll_lane(value, -1))
            kz = jnp.where(tiled(spot == 31, kz), 0.0, kz)
            KXM[here, y] = kxm
            KXP[here, y] = kxp
            KZ[here, y] = kz
            total = (kxm + kxp) + (ka + other) + (kz + roll_lane(kz, 1))
            total = total + (2.0 * scale) * value * (x_wall + tiled(wall, value))
            CD[here, y] = total
            inverse = 1.0 / total
            CI[here, y] = inverse
            CSA[here, y] = CR[here, y] * inverse * (1.0 / CMID)

    blocks(25, setup)

    own = pl.ds(PAD - 2 + 2 * gx, 6)
    CE[...] = CSA[own]

    def sweep(rho, reach, now, later, r_now, r_later):
        rho_next = 1.0 / (2.0 * CSIG - rho)
        step_a = rho_next * rho
        step_b = rho_next * (2.0 / CRAD)
        size = 6 + 2 * reach
        start = PAD + jnp.minimum(jnp.maximum(2 * gx - 2 - reach, 0), planes - size)
        for first in range(0, size, PLANES):
            count = min(PLANES, size - first)
            here = pl.ds(start + first, count)
            prev, after = pl.ds(start + first - 1, count), pl.ds(start + first + 1, count)
            even, odd = now[here, 0], now[here, 1]
            ka, kb = KA[here], KB[here]
            for y, value, beside in (
                (0, even, ka * odd + roll_sub(kb * odd, 1)),
                (1, odd, ka * even + kb * roll_sub(even, -1)),
            ):
                kz = KZ[here, y]
                near = KXM[here, y] * now[prev, y] + KXP[here, y] * now[after, y] + beside
                near = near + (kz * roll_lane(value, -1) + roll_lane(kz * value, 1))
                r = r_now[here, y] - CD[here, y] * value + near
                r_later[here, y] = r
                later[here, y] = tiled(step_a, r) * value + tiled(step_b, r) * (r * CI[here, y])
        CE[...] = CE[...] + later[own]
        return rho_next

    def two(reach):
        def body(_, rho):
            rho = sweep(rho, reach, CSA, CSB, CR, CRB)
            return sweep(rho, reach, CSB, CSA, CRB, CR)

        return body

    rho = jnp.full((8, 128), 1.0 / CSIG, F32)
    for first in range(0, CSWEEPS - 1, 4):
        reach = CSWEEPS - 2 - first
        pairs = min(4, CSWEEPS - 1 - first) // 2
        rho = lax.fori_loop(0, pairs, two(reach), rho)
    if (CSWEEPS - 1) % 2:
        sweep(rho, 0, CSA, CSB, CR, CRB)


def per_device(body_force, phase, viscosity_table, wall_kinds):
    def vmem(*lead):
        return pltpu.VMEM(lead + (8, 128), F32)

    scratch = [
        pltpu.VMEM((16, 16, 8, 128), jnp.int32),
        vmem(6, 12), vmem(8, 4), vmem(8, 14), vmem(6, 12),
        vmem(4, 4), vmem(3, 3), vmem(6, 6), vmem(4, 4),
        vmem(), pltpu.VMEM((16, 2, 32, 128), F32),
    ]
    depth = 2 * NX + 2 * PAD
    scratch += [vmem(depth, 2)] * 4 + [vmem(depth)] * 2 + [vmem(depth, 2)] * 3 + [vmem(depth, 2)] * 3 + [vmem(6, 2)]
    scratch += [vmem(16, 16)]
    for frame in (22, 16, 12):
        scratch += [vmem(frame, frame)] * 12
    n_sems = 107
    scratch += [pltpu.SemaphoreType.DMA((14,)), pltpu.SemaphoreType.DMA((n_sems,)), pltpu.SemaphoreType.DMA((n_sems,))]
    shape = jax.ShapeDtypeStruct(body_force.shape, F32)
    return pl.pallas_call(
        kernel,
        out_shape=(shape, shape),
        in_specs=[
            pl.BlockSpec(memory_space=pl.ANY),
            pl.BlockSpec(memory_space=pl.ANY),
            pl.BlockSpec(memory_space=pltpu.SMEM),
            pl.BlockSpec(memory_space=pltpu.SMEM),
        ],
        out_specs=(pl.BlockSpec(memory_space=pl.ANY), pl.BlockSpec(memory_space=pl.ANY)),
        scratch_shapes=scratch,
        compiler_params=pltpu.CompilerParams(
            collective_id=0, has_side_effects=True, vmem_limit_bytes=56 * 2**20
        ),
        name="vcycle",
    )(body_force, phase, viscosity_table, wall_kinds)


def solution(mesh):
    placed = (P(None, "gx", "gy", None), P("gx", "gy", None), P(), P())
    return jax.shard_map(
        per_device,
        mesh=mesh,
        in_specs=placed,
        out_specs=(P(None, "gx", "gy", None), P(None, "gx", "gy", None)),
        check_vma=False,
    )
```

```python
import jax
import jax.numpy as jnp
from jax import lax
from jax.experimental import pallas as pl
from jax.experimental.pallas import tpu as pltpu
from jax.sharding import PartitionSpec as P


F32 = jnp.float32
MESH = pl.DeviceIdType.MESH
LEVELS = 4
CSWEEPS = 24
NX = 32
NY = 8
LOW, HIGH = 0.2, 2.0
CLOW, CHIGH = 0.05, 2.0

MID = (HIGH + LOW) / 2.0
RAD = (HIGH - LOW) / 2.0
SIG = MID / RAD
RHO0 = 1.0 / SIG
RHO1 = 1.0 / (2.0 * SIG - RHO0)
STEP_A = RHO1 * RHO0
STEP_B = 2.0 * RHO1 / RAD

CMID = (CHIGH + CLOW) / 2.0
CRAD = (CHIGH - CLOW) / 2.0
CSIG = CMID / CRAD

SIDES = [(dx, dy) for dx in (-1, 0, 1) for dy in (-1, 0, 1) if dx or dy]
PAD = 4
BLOCK = 16
PLANES = 8
CHUNK = 8


def lanes():
    return lax.broadcasted_iota(jnp.int32, (8, 128), 1)


def subs():
    return lax.broadcasted_iota(jnp.int32, (8, 128), 0)


def tiled(index, values):
    return jnp.broadcast_to(index, values.shape)


def roll_lane(values, shift):
    return pltpu.roll(values, shift % 128, values.ndim - 1)


def roll_sub(values, shift):
    return pltpu.roll(values, shift % 8, values.ndim - 2)


def pick_lane(values, index):
    return jnp.take_along_axis(values, tiled(index, values), axis=values.ndim - 1, mode="promise_in_bounds")


def choose(mask, one, other):
    return jnp.where(tiled(mask, one), one, other)


def above(values, reach):
    moved = roll_lane(values, -reach)
    return choose(lanes() >= 128 - reach, roll_sub(moved, -1), moved)


def below(values, reach):
    moved = roll_lane(values, reach)
    return choose(lanes() < reach, roll_sub(moved, 1), moved)


def pair_sum(values, reach):
    return values + choose((lanes() & reach) == 0, roll_lane(values, -reach), roll_lane(values, reach))


def spread_sub(values, group):
    kept = jnp.where(tiled(subs() // 2 == group, values), values, 0.0)
    kept = kept + roll_sub(kept, 2)
    return kept + roll_sub(kept, 4)


def by_group(parts):
    group = subs() // 2
    out = parts[3]
    for k in (2, 1, 0):
        out = choose(group == k, parts[k], out)
    return out


def quad(lo, hi):
    return [(j, min(CHUNK, hi - j)) for j in range(lo, hi, CHUNK)]


def loop(lo, hi, body, width=CHUNK):
    whole = isinstance(lo, int) and isinstance(hi, int)
    most = 10
    turns = next(k for k in range(most, 0, -1) if k == 1 or whole and (hi - lo) % k == 0)

    def step(t, carry):
        for k in range(turns):
            body(lo + turns * t + k)
        return carry

    lax.fori_loop(0, (hi - lo) // turns, step, 0)


def clear(ref):
    rows, columns = ref.shape[:2]

    def body(i):
        ref[i] = jnp.zeros((columns, 8, 128), F32)

    loop(0, rows, body)


class Level:
    def __init__(self, index, block, halo, refs):
        self.block, self.halo = block, halo
        self.frame = block + 2 * halo
        self.reach = 2**index
        self.scale = 0.25**index
        self.V, self.KX, self.KY, self.KZ, self.D, self.I, self.R, self.SA, self.SB, self.Q, self.X, self.PR = refs

    def near(self, ref, i, j, m):
        wide = ref[i, pl.ds(j - 1, m + 2)]
        mid = wide[1:-1]
        ky = self.KY[i, pl.ds(j, m + 1)]
        kz = self.KZ[i, pl.ds(j, m)]
        out = self.KX[i, pl.ds(j, m)] * ref[i - 1, pl.ds(j, m)]
        out = out + self.KX[i + 1, pl.ds(j, m)] * ref[i + 1, pl.ds(j, m)]
        out = out + (ky[:-1] * wide[:-2] + ky[1:] * wide[2:])
        out = out + (kz * above(mid, self.reach) + below(kz * mid, self.reach))
        return mid, out

    def build(self, gx, gy, kinds, top, bottom, lo, hi):
        h, b = self.halo, self.block
        half = 0.5 * self.scale
        group, side = subs() // 2, subs() % 2

        def per_kind(wall):
            tile = jnp.zeros((8, 128), F32)
            for c in range(3):
                tile = jnp.where(group == c, kinds[c, wall].astype(F32), tile)
            return tile

        walls = [per_kind(wall) for wall in range(6)]
        z_low = (side == 0) & (lanes() < self.reach)
        z_high = (side == 1) & (lanes() >= 128 - self.reach)
        z_wall = jnp.where(z_low, walls[4], 0.0) + jnp.where(z_high, walls[5], 0.0)
        one, zero = jnp.float32(1.0), jnp.float32(0.0)
        at_x = (jnp.where(gx == 0, one, zero), jnp.where(gx == NX - 1, one, zero))
        at_y = (jnp.where(gy == 0, one, zero), jnp.where(gy == NY - 1, one, zero))

        def faces(i):
            place = gx * b + i - h
            open_x = jnp.where((place == 0) | (place == NX * b), zero, one)
            for j, m in quad(lo, hi):
                here = self.V[i, pl.ds(j, m)]
                self.KX[i, pl.ds(j, m)] = (half * open_x) * (self.V[i - 1, pl.ds(j, m)] + here)

        loop(top, bottom + 1, faces, hi - lo)

        def rest(i):
            x_wall = z_wall + jnp.where(i == h, at_x[0], zero) * walls[0]
            x_wall = x_wall + jnp.where(i == h + b - 1, at_x[1], zero) * walls[1]
            for j, m in quad(lo, hi + 1):
                self.KY[i, pl.ds(j, m)] = half * (self.V[i, pl.ds(j - 1, m)] + self.V[i, pl.ds(j, m)])
            for j, at in ((h, at_y[0]), (h + b, at_y[1])):
                if lo <= j <= hi:
                    self.KY[i, j] = self.KY[i, j] * (one - at)
            for j, m in quad(lo, hi):
                here = self.V[i, pl.ds(j, m)]
                ky = self.KY[i, pl.ds(j, m + 1)]
                kz = half * (here + above(here, self.reach))
                kz = jnp.where(tiled(z_high, kz), 0.0, kz)
                self.KZ[i, pl.ds(j, m)] = kz
                total = self.KX[i, pl.ds(j, m)] + self.KX[i + 1, pl.ds(j, m)] + (ky[:-1] + ky[1:])
                total = total + (kz + below(kz, self.reach))
                self.D[i, pl.ds(j, m)] = total + (2.0 * self.scale) * here * tiled(x_wall, here)
            for j, wall, at in ((h, walls[2], at_y[0]), (h + b - 1, walls[3], at_y[1])):
                if lo <= j < hi:
                    self.D[i, j] = self.D[i, j] + (2.0 * self.scale * at) * self.V[i, j] * wall
            for j, m in quad(lo, hi):
                self.I[i, pl.ds(j, m)] = 1.0 / self.D[i, pl.ds(j, m)]

        loop(top, bottom, rest, hi - lo)

    def first_step(self, src, top, bottom, lo, hi):
        def body(i):
            for j, m in quad(lo, hi):
                self.SA[i, pl.ds(j, m)] = src[i, pl.ds(j, m)] * self.I[i, pl.ds(j, m)] * (1.0 / MID)

        loop(top, bottom, body, hi - lo)

    def second_step(self, src, dst, top, bottom, lo, hi):
        def body(i):
            for j, m in quad(lo, hi):
                step, near = self.near(self.SA, i, j, m)
                r = src[i, pl.ds(j, m)] * (1.0 - 1.0 / MID) + near
                dst[i, pl.ds(j, m)] = r
                self.SB[i, pl.ds(j, m)] = STEP_A * step + STEP_B * (r * self.I[i, pl.ds(j, m)])

        loop(top, bottom, body, hi - lo)

    def third_step(self, top, bottom, lo, hi):
        def body(i):
            for j, m in quad(lo, hi):
                step, near = self.near(self.SB, i, j, m)
                self.Q[i, pl.ds(j, m)] = self.Q[i, pl.ds(j, m)] - self.D[i, pl.ds(j, m)] * step + near
                self.X[i, pl.ds(j, m)] = self.SA[i, pl.ds(j, m)] + step

        loop(top, bottom, body, hi - lo)

    def descend(self, parts=None):
        h, e = self.halo, self.halo + self.block
        parts = parts or (lambda lo, hi, margin: [(lo, hi, lo, hi)])
        for part in parts(h - 2, e + 2, 1):
            self.first_step(self.R, *part)
        for part in parts(h - 1, e + 1, 2):
            self.second_step(self.R, self.Q, *part)
        for part in parts(h, e, 3):
            self.third_step(*part)

    def lift(self, ref, shift, first, count):
        def body(i):
            row = ref[(i + shift[0]) // 2 + shift[1], pl.ds(first, count)]
            row = jnp.broadcast_to(row[:, None], (count, 2, 8, 128)).reshape(2 * count, 8, 128)
            skip = (2 * count - self.frame) // 2
            self.PR[i] = row[skip : skip + self.frame]

        loop(0, self.frame, body)

    def correct(self, lo, hi):
        def body(i):
            for j, m in quad(lo, hi):
                lifted, near = self.near(self.PR, i, j, m)
                q = self.Q[i, pl.ds(j, m)] - self.D[i, pl.ds(j, m)] * lifted + near
                self.R[i, pl.ds(j, m)] = q
                self.SA[i, pl.ds(j, m)] = q * self.I[i, pl.ds(j, m)] * (1.0 / MID)

        loop(lo, hi, body)


def halo_copies(ref, own, halo, cut, corner, gx, gy, send, recv, first, height=6):
    copies = []
    for k, (dx, dy) in enumerate(SIDES):
        src, dst = [], []
        wide = corner if dx and dy else cut
        for d, o, h, w in ((dx, own[0], halo[0], wide[0]), (dy, own[1], halo[1], wide[1])):
            if d == 0:
                src.append(pl.ds(h, o))
                dst.append(pl.ds(h, o))
            elif d < 0:
                src.append(pl.ds(h, w))
                dst.append(pl.ds(h + o, w))
            else:
                src.append(pl.ds(h + o - w, w))
                dst.append(pl.ds(h - w, w))
        target = (lax.rem(gx + dx + NX, NX), lax.rem(gy + dy + NY, NY))
        copies.append(
            pltpu.make_async_remote_copy(
                src_ref=ref.at[src[0], src[1], pl.ds(0, height)],
                dst_ref=ref.at[dst[0], dst[1], pl.ds(0, height)],
                send_sem=send.at[first + k],
                recv_sem=recv.at[first + k],
                device_id=target,
                device_id_type=MESH,
            )
        )
    return copies


def kernel(
    force, phase, table, kinds, out_w, out_r,
    PH, RP1, VP1, QP1, XP1, RP2, VP2, QP2, XP2, MSG, CG, CR, CV, KXM, KXP, KA, KB, KZ, CD, CI, CSA, CSB, CRB, CE, OW, *rest,
):
    refs0, refs1, refs2 = rest[0:12], rest[12:24], rest[24:36]
    in_sem, send, recv = rest[36:]
    gx, gy = lax.axis_index("gx"), lax.axis_index("gy")
    core = lax.rem(gx, 2)
    pair = gx // 2
    L0, L1, L2 = Level(0, 16, 3, refs0), Level(1, 8, 4, refs1), Level(2, 4, 4, refs2)
    group, side, lane = subs() // 2, subs() % 2, lanes()

    loads = []
    for c in range(3):
        for s in range(2):
            loads.append(
                pltpu.make_async_copy(
                    force.at[c, :, :, pl.ds(128 * s, 128)],
                    L0.R.at[pl.ds(3, 16), pl.ds(3, 16), 2 * c + s],
                    in_sem.at[len(loads)],
                )
            )
    for c in range(4):
        for s in range(2):
            loads.append(
                pltpu.make_async_copy(
                    phase.at[:, :, pl.ds(128 * s, 128)], PH.at[:, :, 2 * c + s], in_sem.at[len(loads)]
                )
            )
    for copy in loads:
        copy.start()

    for ref in (RP1, QP1, XP1, RP2, QP2, XP2, L0.Q):
        clear(ref)

    partners = [(lax.rem(gx + dx + NX, NX), lax.rem(gy + dy + NY, NY)) for dx, dy in SIDES]
    partners += [(gx, lax.rem(gy + k, NY)) for k in range(2, 7)]
    partners += [(lax.rem(gx + 2 * k, NX), gy) for k in range(1, 16)]
    barrier = pltpu.get_barrier_semaphore()
    for partner in partners:
        pl.semaphore_signal(barrier, inc=1, device_id=partner, device_id_type=MESH)

    values = jnp.zeros((8, 128), F32)
    for k in range(8):
        values = jnp.where(lane == k, table[k], values)
    for copy in loads:
        copy.wait()

    def look_up(i):
        for j, m in quad(0, 16):
            index = PH[i, pl.ds(j, m)]
            cells = pick_lane(jnp.broadcast_to(values, index.shape), index)
            L0.V[i + 3, pl.ds(j + 3, m)] = cells
            L0.R[i + 3, pl.ds(j + 3, m)] = choose(group == 3, cells, L0.R[i + 3, pl.ds(j + 3, m)])

    loop(0, 16, look_up)
    pl.semaphore_wait(barrier, len(partners))

    pending = halo_copies(L0.R, (16, 16), (3, 3), (2, 2), (2, 2), gx, gy, send, recv, 0, 8)
    for k, (dx, dy) in enumerate(((-1, 0), (1, 0), (0, -1), (0, 1))):
        span = {0: (pl.ds(3, 16), pl.ds(3, 16)), -1: (pl.ds(5, 1), pl.ds(21, 1)), 1: (pl.ds(16, 1), pl.ds(0, 1))}
        pending.append(
            pltpu.make_async_remote_copy(
                src_ref=L0.R.at[span[dx][0], span[dy][0], pl.ds(6, 2)],
                dst_ref=L0.R.at[span[dx][1], span[dy][1], pl.ds(6, 2)],
                send_sem=send.at[8 + k],
                recv_sem=recv.at[8 + k],
                device_id=(lax.rem(gx + dx + NX, NX), lax.rem(gy + dy + NY, NY)),
                device_id_type=MESH,
            )
        )
    for copy in pending:
        copy.start()
    faces = pending
    sent = []

    def restrict(src, halo_src, count, reach, i):
        row = src[halo_src + 2 * i, pl.ds(halo_src, count)] + src[halo_src + 2 * i + 1, pl.ds(halo_src, count)]
        row = row.reshape(count // 2, 2, 8, 128)
        return pair_sum(row[:, 0] + row[:, 1], reach) * 0.125

    def coarsen_v1(i):
        L1.V[4 + i, pl.ds(4, 8)] = restrict(L0.V, 3, 16, 1, i)

    def coarsen_v2(i):
        L2.V[4 + i, pl.ds(4, 4)] = restrict(L1.V, 4, 8, 2, i)

    loop(0, 8, coarsen_v1)
    loop(0, 4, coarsen_v2)

    def pack_v1(a):
        for b in range(2):
            parts = [by_group([L1.V[4 + 2 * a + p, 4 + 4 * b + k] for k in range(4)]) for p in range(2)]
            VP1[a + 2, b + 1] = jnp.where(lane % 2 == 0, parts[0], parts[1])

    loop(0, 4, pack_v1)
    tile = None
    for p in range(4):
        part = by_group([L2.V[4 + p, 4 + k] for k in range(4)])
        tile = part if tile is None else jnp.where(lane % 4 == p, part, tile)
    VP2[1, 1] = tile

    def inside(lo, hi, margin):
        return [(3 + margin, 19 - margin, 3 + margin, 19 - margin)]

    def around(lo, hi, margin):
        a, b = 3 + margin, 19 - margin
        return [(lo, a, lo, hi), (b, hi, lo, hi), (a, b, lo, a), (a, b, b, hi)]

    for part in inside(1, 21, 1):
        L0.build(gx, gy, kinds, *part)
    L0.descend(inside)
    for copy in pending:
        copy.wait_recv()

    early = halo_copies(VP1, (4, 2), (2, 1), (2, 1), (2, 1), gx, gy, send, recv, 12, 8)
    early += halo_copies(VP2, (1, 1), (1, 1), (1, 1), (1, 1), gx, gy, send, recv, 20, 8)
    for copy in early:
        copy.start()
    sent += early

    for top, bottom, lo, hi in around(0, 22, 0):

        def fill_v0(i):
            for j, m in quad(lo, hi):
                L0.V[i, pl.ds(j, m)] = spread_sub(L0.R[i, pl.ds(j, m)], 3)

        loop(top, bottom, fill_v0, hi - lo)
    for part in around(1, 21, 1):
        L0.build(gx, gy, kinds, *part)
    L0.descend(around)
    for copy in faces:
        copy.wait_send()

    def pack_r1(a):
        one, other = restrict(L0.Q, 3, 16, 1, 2 * a), restrict(L0.Q, 3, 16, 1, 2 * a + 1)
        RP1[a + 1, pl.ds(2, 8)] = choose(lane % 2 == 0, one, other)

    loop(0, 4, pack_r1)
    pending = halo_copies(RP1, (4, 8), (1, 2), (1, 2), (1, 1), gx, gy, send, recv, 28)
    for copy in pending:
        copy.start()
    sent += pending
    for copy in early:
        copy.wait_recv()

    def unpack_v1(a):
        for b in range(4):
            both = VP1[a, b]
            for p in range(2):
                part = pick_lane(both, (lane // 2) * 2 + p)
                for k in range(4):
                    L1.V[2 * a + p, 4 * b + k] = spread_sub(part, k)

    loop(0, 8, unpack_v1)

    def unpack_v2(a):
        for b in range(3):
            both = VP2[a, b]
            for p in range(4):
                part = pick_lane(both, (lane // 4) * 4 + p)
                for k in range(4):
                    L2.V[4 * a + p, 4 * b + k] = spread_sub(part, k)

    loop(0, 3, unpack_v2)
    L1.build(gx, gy, kinds, 1, 15, 1, 15)
    L2.build(gx, gy, kinds, 1, 11, 1, 11)
    for copy in pending:
        copy.wait_recv()

    def unpack_pairs(src, dst, count, x_first, y_first, y_count):
        def body(a):
            row = src[a, pl.ds(0, y_count)]
            for p in range(2):
                dst[x_first + 2 * a + p, pl.ds(y_first, y_count)] = pick_lane(row, (lane // 2) * 2 + p)

        loop(0, count, body)

    unpack_pairs(RP1, L1.R, 6, 2, 2, 12)
    L1.descend()

    def pack_r2(a):
        rows = []
        for p in range(2):
            row = restrict(L1.Q, 4, 8, 2, 2 * a + p).reshape(2, 2, 8, 128)
            rows.append(choose(lane % 2 == 0, row[:, 0], row[:, 1]))
        RP2[a + 1, pl.ds(1, 2)] = choose(lane % 4 < 2, rows[0], rows[1])

    loop(0, 2, pack_r2)
    pending = halo_copies(RP2, (2, 2), (1, 1), (1, 1), (1, 1), gx, gy, send, recv, 36)
    for copy in pending:
        copy.start()
    sent += pending
    late0 = halo_copies(L0.Q, (16, 16), (3, 3), (2, 2), (1, 1), gx, gy, send, recv, 99)
    for copy in late0:
        copy.start()
    sent += late0
    for copy in pending:
        copy.wait_recv()

    def unpack_quads(src, dst, count, first):
        def body(a):
            for b in range(count):
                both = src[a, b]
                for p in range(2):
                    for k in range(2):
                        dst[first + 2 * a + p, first + 2 * b + k] = pick_lane(both, (lane // 4) * 4 + (2 * p + k))

        loop(0, count, body)

    unpack_quads(RP2, L2.R, 4, 2)
    L2.descend()

    for p in range(2):
        r3 = restrict(L2.Q, 4, 4, 4, p)
        v3 = restrict(L2.V, 4, 4, 4, p)
        both = choose(group == 3, v3, r3)
        both = pick_lane(both, 8 * (lane % 16))
        both = jnp.where(tiled(lane // 16 == subs(), both), both, 0.0)
        for k in range(2):
            MSG[pl.ds(2 * p + k, 1), :] = jnp.sum(both[k], axis=0, keepdims=True)
    rows = pl.ds(pl.multiple_of(4 * gy, 4), 4)
    keep = pltpu.make_async_copy(MSG.at[pl.ds(0, 4)], CG.at[pair, core, rows], in_sem.at[0])
    keep.start()
    pending = []
    for k in range(1, 16):
        pending.append(
            pltpu.make_async_remote_copy(
                src_ref=MSG.at[pl.ds(0, 4)],
                dst_ref=CG.at[pair, core, rows],
                send_sem=send.at[44 + k - 1],
                recv_sem=recv.at[44 + k - 1],
                device_id=(lax.rem(gx + 2 * k, NX), gy),
                device_id_type=MESH,
            )
        )
    for copy in pending:
        copy.start()
    sent += pending

    def pack_1(a):
        for src, dst, x0, y0 in ((L1.Q, QP1, 2, 3), (L1.X, XP1, 1, 2)):
            one, other = src[4 + 2 * a, pl.ds(4, 8)], src[5 + 2 * a, pl.ds(4, 8)]
            dst[x0 + a, pl.ds(y0, 8)] = choose(lane % 2 == 0, one, other)

    loop(0, 4, pack_1)

    def pack_2(a):
        for src, dst, x0 in ((L2.Q, QP2, 2), (L2.X, XP2, 1)):
            mixed = []
            for p in range(2):
                row = src[4 + 2 * a + p, pl.ds(4, 4)].reshape(2, 2, 8, 128)
                mixed.append(choose(lane % 2 == 0, row[:, 0], row[:, 1]))
            dst[x0 + a, pl.ds(x0, 2)] = choose(lane % 4 < 2, mixed[0], mixed[1])

    loop(0, 2, pack_2)
    late2 = halo_copies(QP2, (2, 2), (2, 2), (2, 2), (2, 2), gx, gy, send, recv, 67)
    late2 += halo_copies(XP2, (2, 2), (1, 1), (1, 1), (1, 1), gx, gy, send, recv, 75)
    late1 = halo_copies(QP1, (4, 8), (2, 3), (2, 3), (1, 2), gx, gy, send, recv, 83)
    late1 += halo_copies(XP1, (4, 8), (1, 2), (1, 2), (1, 1), gx, gy, send, recv, 91)
    keep.wait()
    for copy in pending:
        copy.wait_recv()

    pending = []
    for k in range(1, 8):
        pending.append(
            pltpu.make_async_remote_copy(
                src_ref=CG.at[:, core, rows],
                dst_ref=CG.at[:, core, rows],
                send_sem=send.at[59 + k - 1],
                recv_sem=recv.at[59 + k - 1],
                device_id=(gx, lax.rem(gy + k, NY)),
                device_id_type=MESH,
            )
        )
    for copy in pending:
        copy.start()
    sent += pending
    for copy in pending:
        copy.wait_recv()
    swap = pltpu.make_async_remote_copy(
        src_ref=CG.at[:, core],
        dst_ref=CG.at[:, core],
        send_sem=send.at[66],
        recv_sem=recv.at[66],
        device_id=(gx + 1 - 2 * core, gy),
        device_id_type=MESH,
    )
    swap.start()
    sent.append(swap)
    for copy in late2 + late1:
        copy.start()
    sent += late2 + late1
    swap.wait_recv()

    coarse(gx, gy, kinds, CG, CR, CV, KXM, KXP, KA, KB, KZ, CD, CI, CSA, CSB, CRB, CE)

    flat = CE.reshape(96, 128)

    def expand(a):
        for j in range(6):
            row = 16 * a + 8 * (j % 2) + lax.rem(gy + 7 + j // 2, 8)
            both = jnp.broadcast_to(flat[pl.ds(row, 1), :], (8, 128))
            both = pick_lane(both, 16 * subs() + lane // 8)
            for p in range(2):
                for k in range(2):
                    L2.PR[2 * a + p, 2 * j + k] = both

    loop(0, 6, expand)

    for copy in late2:
        copy.wait_recv()
    unpack_quads(QP2, L2.Q, 6, 0)
    unpack_quads(XP2, L2.X, 4, 2)

    def middle(level):
        h, b = level.halo, level.block
        level.correct(h - 3, h + b + 3)
        level.second_step(level.R, level.R, h - 2, h + b + 2, h - 2, h + b + 2)

        def body(i):
            for j, m in quad(h - 2, h + b + 2):
                here = pl.ds(j, m)
                level.SB[i, here] = (level.X[i, here] + level.PR[i, here]) + (level.SA[i, here] + level.SB[i, here])

        loop(h - 2, h + b + 2, body)

    middle(L2)
    L1.lift(L2.SB, (0, 2), 2, 8)
    for copy in late1:
        copy.wait_recv()

    def unpack_q1(a):
        row = QP1[a]
        for p in range(2):
            L1.Q[2 * a + p, pl.ds(1, 14)] = pick_lane(row, (lane // 2) * 2 + p)

    loop(0, 8, unpack_q1)
    unpack_pairs(XP1, L1.X, 6, 2, 2, 12)
    middle(L1)
    L0.lift(L1.SB, (1, 2), 2, 12)
    for copy in late0:
        copy.wait_recv()
    L0.correct(1, 21)
    L0.second_step(L0.R, L0.R, 2, 20, 2, 20)

    def last(i):
        for j, m in quad(3, 19):
            here = pl.ds(j, m)
            step, near = L0.near(L0.SB, i, j, m)
            diag = L0.D[i, here]
            field = (L0.X[i, here] + L0.PR[i, here]) + (L0.SA[i, here] + step)
            L0.R[i, here] = L0.R[i, here] - diag * step + near
            OW[i - 3, pl.ds(j - 3, m)] = diag * field

    loop(3, 19, last)
    stores = []
    for c in range(3):
        for s in range(2):
            place = pl.ds(128 * s, 128)
            stores.append(
                pltpu.make_async_copy(OW.at[:, :, 2 * c + s], out_w.at[c, :, :, place], in_sem.at[len(stores)])
            )
            stores.append(
                pltpu.make_async_copy(
                    L0.R.at[pl.ds(3, 16), pl.ds(3, 16), 2 * c + s],
                    out_r.at[c, :, :, place],
                    in_sem.at[len(stores)],
                )
            )
    for copy in stores:
        copy.start()
    for copy in sent:
        copy.wait_send()
    for copy in stores:
        copy.wait()


def coarse(gx, gy, kinds, CG, CR, CV, KXM, KXP, KA, KB, KZ, CD, CI, CSA, CSB, CRB, CE):
    planes = 2 * NX
    scale = 0.25 ** (LEVELS - 1)
    lane = lanes()
    spot = lane % 32
    flat = CG.reshape(1024, 128)

    def blocks(reach, body):
        lo = jnp.maximum(2 * gx - 2 - reach, 0) // BLOCK
        hi = (jnp.minimum(2 * gx + 4 + reach, planes) + BLOCK - 1) // BLOCK
        loop(lo, hi, body)

    zeros = jnp.zeros((PAD, 2, 8, 128), F32)
    for place in (0, PAD + planes):
        CV[pl.ds(place, PAD)] = zeros
        CSA[pl.ds(place, PAD)] = zeros
        CSB[pl.ds(place, PAD)] = zeros

    def take(b):
        for q in range(BLOCK):
            for y in range(2):
                start = 16 * BLOCK * b + 32 * (q // 2) + 2 * (q % 2) + y
                row = flat[pl.ds(start, 8, stride=4), :]
                CR[PAD + BLOCK * b + q, y] = row
                CV[PAD + BLOCK * b + q, y] = pick_lane(row, 96 + spot)

    blocks(26, take)

    def per_kind(wall):
        tile = jnp.zeros((8, 128), F32)
        for c in range(3):
            tile = jnp.where(lane // 32 == c, kinds[c, wall].astype(F32), tile)
        return tile

    walls = [per_kind(wall) for wall in range(6)]
    z_wall = jnp.where(spot == 0, walls[4], 0.0) + jnp.where(spot == 31, walls[5], 0.0)
    low_y = z_wall + jnp.where(subs() == 0, walls[2], 0.0)
    high_y = z_wall + jnp.where(subs() == 7, walls[3], 0.0)

    def setup(b):
        here = pl.ds(PAD + BLOCK * b, BLOCK)
        prev, after = pl.ds(PAD - 1 + BLOCK * b, BLOCK), pl.ds(PAD + 1 + BLOCK * b, BLOCK)
        plane = lax.broadcasted_iota(jnp.int32, (BLOCK, 8, 128), 0) + BLOCK * b
        even, odd = CV[here, 0], CV[here, 1]
        half = 0.5 * scale
        ka = half * (even + odd)
        kb = half * (odd + roll_sub(even, -1))
        kb = jnp.where(tiled(subs() == 7, kb), 0.0, kb)
        KA[here] = ka
        KB[here] = kb
        x_wall = jnp.where(plane == 0, tiled(walls[0], even), 0.0)
        x_wall = x_wall + jnp.where(plane == planes - 1, tiled(walls[1], even), 0.0)
        for y, value, wall, other in ((0, even, low_y, roll_sub(kb, 1)), (1, odd, high_y, kb)):
            kxm = jnp.where(plane == 0, 0.0, half * (CV[prev, y] + value))
            kxp = jnp.where(plane == planes - 1, 0.0, half * (value + CV[after, y]))
            kz = half * (value + roll_lane(value, -1))
            kz = jnp.where(tiled(spot == 31, kz), 0.0, kz)
            KXM[here, y] = kxm
            KXP[here, y] = kxp
            KZ[here, y] = kz
            total = (kxm + kxp) + (ka + other) + (kz + roll_lane(kz, 1))
            total = total + (2.0 * scale) * value * (x_wall + tiled(wall, value))
            CD[here, y] = total
            inverse = 1.0 / total
            CI[here, y] = inverse
            CSA[here, y] = CR[here, y] * inverse * (1.0 / CMID)

    blocks(25, setup)

    own = pl.ds(PAD - 2 + 2 * gx, 6)
    CE[...] = CSA[own]

    def sweep(rho, reach, now, later, r_now, r_later):
        rho_next = 1.0 / (2.0 * CSIG - rho)
        step_a = rho_next * rho
        step_b = rho_next * (2.0 / CRAD)
        size = 6 + 2 * reach
        start = PAD + jnp.minimum(jnp.maximum(2 * gx - 2 - reach, 0), planes - size)
        for first in range(0, size, PLANES):
            count = min(PLANES, size - first)
            here = pl.ds(start + first, count)
            prev, after = pl.ds(start + first - 1, count), pl.ds(start + first + 1, count)
            even, odd = now[here, 0], now[here, 1]
            ka, kb = KA[here], KB[here]
            for y, value, beside in (
                (0, even, ka * odd + roll_sub(kb * odd, 1)),
                (1, odd, ka * even + kb * roll_sub(even, -1)),
            ):
                kz = KZ[here, y]
                near = KXM[here, y] * now[prev, y] + KXP[here, y] * now[after, y] + beside
                near = near + (kz * roll_lane(value, -1) + roll_lane(kz * value, 1))
                r = r_now[here, y] - CD[here, y] * value + near
                r_later[here, y] = r
                later[here, y] = tiled(step_a, r) * value + tiled(step_b, r) * (r * CI[here, y])
        CE[...] = CE[...] + later[own]
        return rho_next

    def two(reach):
        def body(_, rho):
            rho = sweep(rho, reach, CSA, CSB, CR, CRB)
            return sweep(rho, reach, CSB, CSA, CRB, CR)

        return body

    rho = jnp.full((8, 128), 1.0 / CSIG, F32)
    for first in range(0, CSWEEPS - 1, 4):
        reach = CSWEEPS - 2 - first
        pairs = min(4, CSWEEPS - 1 - first) // 2
        rho = lax.fori_loop(0, pairs, two(reach), rho)
    if (CSWEEPS - 1) % 2:
        sweep(rho, 0, CSA, CSB, CR, CRB)


def per_device(body_force, phase, viscosity_table, wall_kinds):
    def vmem(*lead):
        return pltpu.VMEM(lead + (8, 128), F32)

    scratch = [
        pltpu.VMEM((16, 16, 8, 128), jnp.int32),
        vmem(6, 12), vmem(8, 4), vmem(8, 14), vmem(6, 12),
        vmem(4, 4), vmem(3, 3), vmem(6, 6), vmem(4, 4),
        vmem(), pltpu.VMEM((16, 2, 32, 128), F32),
    ]
    depth = 2 * NX + 2 * PAD
    scratch += [vmem(depth, 2)] * 4 + [vmem(depth)] * 2 + [vmem(depth, 2)] * 3 + [vmem(depth, 2)] * 3 + [vmem(6, 2)]
    scratch += [vmem(16, 16)]
    for frame in (22, 16, 12):
        scratch += [vmem(frame, frame)] * 12
    n_sems = 107
    scratch += [pltpu.SemaphoreType.DMA((14,)), pltpu.SemaphoreType.DMA((n_sems,)), pltpu.SemaphoreType.DMA((n_sems,))]
    shape = jax.ShapeDtypeStruct(body_force.shape, F32)
    return pl.pallas_call(
        kernel,
        out_shape=(shape, shape),
        in_specs=[
            pl.BlockSpec(memory_space=pl.ANY),
            pl.BlockSpec(memory_space=pl.ANY),
            pl.BlockSpec(memory_space=pltpu.SMEM),
            pl.BlockSpec(memory_space=pltpu.SMEM),
        ],
        out_specs=(pl.BlockSpec(memory_space=pl.ANY), pl.BlockSpec(memory_space=pl.ANY)),
        scratch_shapes=scratch,
        compiler_params=pltpu.CompilerParams(
            collective_id=0, has_side_effects=True, vmem_limit_bytes=56 * 2**20
        ),
        name="vcycle",
    )(body_force, phase, viscosity_table, wall_kinds)


def solution(mesh):
    placed = (P(None, "gx", "gy", None), P("gx", "gy", None), P(), P())
    return jax.shard_map(
        per_device,
        mesh=mesh,
        in_specs=placed,
        out_specs=(P(None, "gx", "gy", None), P(None, "gx", "gy", None)),
        check_vma=False,
    )
```

```python
import jax
import jax.numpy as jnp
from jax import lax
from jax.experimental import pallas as pl
from jax.experimental.pallas import tpu as pltpu
from jax.sharding import PartitionSpec as P


F32 = jnp.float32
MESH = pl.DeviceIdType.MESH
LEVELS = 4
CSWEEPS = 24
NX = 32
NY = 8
LOW, HIGH = 0.2, 2.0
CLOW, CHIGH = 0.05, 2.0

MID = (HIGH + LOW) / 2.0
RAD = (HIGH - LOW) / 2.0
SIG = MID / RAD
RHO0 = 1.0 / SIG
RHO1 = 1.0 / (2.0 * SIG - RHO0)
STEP_A = RHO1 * RHO0
STEP_B = 2.0 * RHO1 / RAD

CMID = (CHIGH + CLOW) / 2.0
CRAD = (CHIGH - CLOW) / 2.0
CSIG = CMID / CRAD

SIDES = [(dx, dy) for dx in (-1, 0, 1) for dy in (-1, 0, 1) if dx or dy]
PAD = 4
BLOCK = 16
PLANES = 8
CHUNK = 8


def lanes():
    return lax.broadcasted_iota(jnp.int32, (8, 128), 1)


def subs():
    return lax.broadcasted_iota(jnp.int32, (8, 128), 0)


def tiled(index, values):
    return jnp.broadcast_to(index, values.shape)


def roll_lane(values, shift):
    return pltpu.roll(values, shift % 128, values.ndim - 1)


def roll_sub(values, shift):
    return pltpu.roll(values, shift % 8, values.ndim - 2)


def pick_lane(values, index):
    return jnp.take_along_axis(values, tiled(index, values), axis=values.ndim - 1, mode="promise_in_bounds")


def choose(mask, one, other):
    return jnp.where(tiled(mask, one), one, other)


def above(values, reach):
    moved = roll_lane(values, -reach)
    return choose(lanes() >= 128 - reach, roll_sub(moved, -1), moved)


def below(values, reach):
    moved = roll_lane(values, reach)
    return choose(lanes() < reach, roll_sub(moved, 1), moved)


def pair_sum(values, reach):
    return values + choose((lanes() & reach) == 0, roll_lane(values, -reach), roll_lane(values, reach))


def spread_sub(values, group):
    kept = jnp.where(tiled(subs() // 2 == group, values), values, 0.0)
    kept = kept + roll_sub(kept, 2)
    return kept + roll_sub(kept, 4)


def by_group(parts):
    group = subs() // 2
    out = parts[3]
    for k in (2, 1, 0):
        out = choose(group == k, parts[k], out)
    return out


def quad(lo, hi):
    return [(j, min(CHUNK, hi - j)) for j in range(lo, hi, CHUNK)]


def loop(lo, hi, body, width=CHUNK):
    whole = isinstance(lo, int) and isinstance(hi, int)
    most = 10
    turns = next(k for k in range(most, 0, -1) if k == 1 or whole and (hi - lo) % k == 0)

    def step(t, carry):
        for k in range(turns):
            body(lo + turns * t + k)
        return carry

    lax.fori_loop(0, (hi - lo) // turns, step, 0)


def clear(ref):
    rows, columns = ref.shape[:2]

    def body(i):
        ref[i] = jnp.zeros((columns, 8, 128), F32)

    loop(0, rows, body)


class Level:
    def __init__(self, index, block, halo, refs):
        self.block, self.halo = block, halo
        self.frame = block + 2 * halo
        self.reach = 2**index
        self.scale = 0.25**index
        self.V, self.KX, self.KY, self.KZ, self.D, self.I, self.R, self.SA, self.SB, self.Q, self.X, self.PR = refs

    def near(self, ref, i, j, m):
        wide = ref[i, pl.ds(j - 1, m + 2)]
        mid = wide[1:-1]
        ky = self.KY[i, pl.ds(j, m + 1)]
        kz = self.KZ[i, pl.ds(j, m)]
        out = self.KX[i, pl.ds(j, m)] * ref[i - 1, pl.ds(j, m)]
        out = out + self.KX[i + 1, pl.ds(j, m)] * ref[i + 1, pl.ds(j, m)]
        out = out + (ky[:-1] * wide[:-2] + ky[1:] * wide[2:])
        out = out + (kz * above(mid, self.reach) + below(kz * mid, self.reach))
        return mid, out

    def build(self, gx, gy, kinds, top, bottom, lo, hi):
        h, b = self.halo, self.block
        half = 0.5 * self.scale
        group, side = subs() // 2, subs() % 2

        def per_kind(wall):
            tile = jnp.zeros((8, 128), F32)
            for c in range(3):
                tile = jnp.where(group == c, kinds[c, wall].astype(F32), tile)
            return tile

        walls = [per_kind(wall) for wall in range(6)]
        z_low = (side == 0) & (lanes() < self.reach)
        z_high = (side == 1) & (lanes() >= 128 - self.reach)
        z_wall = jnp.where(z_low, walls[4], 0.0) + jnp.where(z_high, walls[5], 0.0)
        one, zero = jnp.float32(1.0), jnp.float32(0.0)
        at_x = (jnp.where(gx == 0, one, zero), jnp.where(gx == NX - 1, one, zero))
        at_y = (jnp.where(gy == 0, one, zero), jnp.where(gy == NY - 1, one, zero))

        def faces(i):
            place = gx * b + i - h
            open_x = jnp.where((place == 0) | (place == NX * b), zero, one)
            for j, m in quad(lo, hi):
                here = self.V[i, pl.ds(j, m)]
                self.KX[i, pl.ds(j, m)] = (half * open_x) * (self.V[i - 1, pl.ds(j, m)] + here)

        loop(top, bottom + 1, faces, hi - lo)

        def rest(i):
            x_wall = z_wall + jnp.where(i == h, at_x[0], zero) * walls[0]
            x_wall = x_wall + jnp.where(i == h + b - 1, at_x[1], zero) * walls[1]
            for j, m in quad(lo, hi + 1):
                self.KY[i, pl.ds(j, m)] = half * (self.V[i, pl.ds(j - 1, m)] + self.V[i, pl.ds(j, m)])
            for j, at in ((h, at_y[0]), (h + b, at_y[1])):
                if lo <= j <= hi:
                    self.KY[i, j] = self.KY[i, j] * (one - at)
            for j, m in quad(lo, hi):
                here = self.V[i, pl.ds(j, m)]
                ky = self.KY[i, pl.ds(j, m + 1)]
                kz = half * (here + above(here, self.reach))
                kz = jnp.where(tiled(z_high, kz), 0.0, kz)
                self.KZ[i, pl.ds(j, m)] = kz
                total = self.KX[i, pl.ds(j, m)] + self.KX[i + 1, pl.ds(j, m)] + (ky[:-1] + ky[1:])
                total = total + (kz + below(kz, self.reach))
                self.D[i, pl.ds(j, m)] = total + (2.0 * self.scale) * here * tiled(x_wall, here)
            for j, wall, at in ((h, walls[2], at_y[0]), (h + b - 1, walls[3], at_y[1])):
                if lo <= j < hi:
                    self.D[i, j] = self.D[i, j] + (2.0 * self.scale * at) * self.V[i, j] * wall
            for j, m in quad(lo, hi):
                self.I[i, pl.ds(j, m)] = 1.0 / self.D[i, pl.ds(j, m)]

        loop(top, bottom, rest, hi - lo)

    def first_step(self, src, top, bottom, lo, hi):
        def body(i):
            for j, m in quad(lo, hi):
                self.SA[i, pl.ds(j, m)] = src[i, pl.ds(j, m)] * self.I[i, pl.ds(j, m)] * (1.0 / MID)

        loop(top, bottom, body, hi - lo)

    def second_step(self, src, dst, top, bottom, lo, hi):
        def body(i):
            for j, m in quad(lo, hi):
                step, near = self.near(self.SA, i, j, m)
                r = src[i, pl.ds(j, m)] * (1.0 - 1.0 / MID) + near
                dst[i, pl.ds(j, m)] = r
                self.SB[i, pl.ds(j, m)] = STEP_A * step + STEP_B * (r * self.I[i, pl.ds(j, m)])

        loop(top, bottom, body, hi - lo)

    def third_step(self, top, bottom, lo, hi):
        def body(i):
            for j, m in quad(lo, hi):
                step, near = self.near(self.SB, i, j, m)
                self.Q[i, pl.ds(j, m)] = self.Q[i, pl.ds(j, m)] - self.D[i, pl.ds(j, m)] * step + near
                self.X[i, pl.ds(j, m)] = self.SA[i, pl.ds(j, m)] + step

        loop(top, bottom, body, hi - lo)

    def descend(self, parts=None):
        h, e = self.halo, self.halo + self.block
        parts = parts or (lambda lo, hi, margin: [(lo, hi, lo, hi)])
        for part in parts(h - 2, e + 2, 1):
            self.first_step(self.R, *part)
        for part in parts(h - 1, e + 1, 2):
            self.second_step(self.R, self.Q, *part)
        for part in parts(h, e, 3):
            self.third_step(*part)

    def lift(self, ref, shift, first, count):
        def body(i):
            row = ref[(i + shift[0]) // 2 + shift[1], pl.ds(first, count)]
            row = jnp.broadcast_to(row[:, None], (count, 2, 8, 128)).reshape(2 * count, 8, 128)
            skip = (2 * count - self.frame) // 2
            self.PR[i] = row[skip : skip + self.frame]

        loop(0, self.frame, body)

    def correct(self, lo, hi):
        def body(i):
            for j, m in quad(lo, hi):
                lifted, near = self.near(self.PR, i, j, m)
                q = self.Q[i, pl.ds(j, m)] - self.D[i, pl.ds(j, m)] * lifted + near
                self.R[i, pl.ds(j, m)] = q
                self.SA[i, pl.ds(j, m)] = q * self.I[i, pl.ds(j, m)] * (1.0 / MID)

        loop(lo, hi, body)


def halo_copies(ref, own, halo, cut, corner, gx, gy, send, recv, first, height=6):
    copies = []
    for k, (dx, dy) in enumerate(SIDES):
        src, dst = [], []
        wide = corner if dx and dy else cut
        for d, o, h, w in ((dx, own[0], halo[0], wide[0]), (dy, own[1], halo[1], wide[1])):
            if d == 0:
                src.append(pl.ds(h, o))
                dst.append(pl.ds(h, o))
            elif d < 0:
                src.append(pl.ds(h, w))
                dst.append(pl.ds(h + o, w))
            else:
                src.append(pl.ds(h + o - w, w))
                dst.append(pl.ds(h - w, w))
        target = (lax.rem(gx + dx + NX, NX), lax.rem(gy + dy + NY, NY))
        copies.append(
            pltpu.make_async_remote_copy(
                src_ref=ref.at[src[0], src[1], pl.ds(0, height)],
                dst_ref=ref.at[dst[0], dst[1], pl.ds(0, height)],
                send_sem=send.at[first + k],
                recv_sem=recv.at[first + k],
                device_id=target,
                device_id_type=MESH,
            )
        )
    return copies


def kernel(
    force, phase, table, kinds, out_w, out_r,
    PH, RP1, VP1, QP1, XP1, RP2, VP2, QP2, XP2, MSG, CG, CR, CV, KXM, KXP, KA, KB, KZ, CD, CI, CSA, CSB, CRB, CE, OW, *rest,
):
    refs0, refs1, refs2 = rest[0:12], rest[12:24], rest[24:36]
    in_sem, send, recv = rest[36:]
    gx, gy = lax.axis_index("gx"), lax.axis_index("gy")
    core = lax.rem(gx, 2)
    pair = gx // 2
    L0, L1, L2 = Level(0, 16, 3, refs0), Level(1, 8, 4, refs1), Level(2, 4, 4, refs2)
    group, side, lane = subs() // 2, subs() % 2, lanes()

    loads = []
    for c in range(3):
        for s in range(2):
            loads.append(
                pltpu.make_async_copy(
                    force.at[c, :, :, pl.ds(128 * s, 128)],
                    L0.R.at[pl.ds(3, 16), pl.ds(3, 16), 2 * c + s],
                    in_sem.at[len(loads)],
                )
            )
    for c in range(4):
        for s in range(2):
            loads.append(
                pltpu.make_async_copy(
                    phase.at[:, :, pl.ds(128 * s, 128)], PH.at[:, :, 2 * c + s], in_sem.at[len(loads)]
                )
            )
    for copy in loads:
        copy.start()

    for ref in (RP1, QP1, XP1, RP2, QP2, XP2, L0.Q):
        clear(ref)

    partners = [(lax.rem(gx + dx + NX, NX), lax.rem(gy + dy + NY, NY)) for dx, dy in SIDES]
    partners += [(gx, lax.rem(gy + k, NY)) for k in range(2, 7)]
    partners += [(lax.rem(gx + 2 * k, NX), gy) for k in range(1, 16)]
    barrier = pltpu.get_barrier_semaphore()
    for partner in partners:
        pl.semaphore_signal(barrier, inc=1, device_id=partner, device_id_type=MESH)

    values = jnp.zeros((8, 128), F32)
    for k in range(8):
        values = jnp.where(lane == k, table[k], values)
    for copy in loads:
        copy.wait()

    def look_up(i):
        for j, m in quad(0, 16):
            index = PH[i, pl.ds(j, m)]
            cells = pick_lane(jnp.broadcast_to(values, index.shape), index)
            L0.V[i + 3, pl.ds(j + 3, m)] = cells
            L0.R[i + 3, pl.ds(j + 3, m)] = choose(group == 3, cells, L0.R[i + 3, pl.ds(j + 3, m)])

    loop(0, 16, look_up)
    pl.semaphore_wait(barrier, len(partners))

    pending = halo_copies(L0.R, (16, 16), (3, 3), (2, 2), (2, 2), gx, gy, send, recv, 0, 8)
    for k, (dx, dy) in enumerate(((-1, 0), (1, 0), (0, -1), (0, 1))):
        span = {0: (pl.ds(3, 16), pl.ds(3, 16)), -1: (pl.ds(5, 1), pl.ds(21, 1)), 1: (pl.ds(16, 1), pl.ds(0, 1))}
        pending.append(
            pltpu.make_async_remote_copy(
                src_ref=L0.R.at[span[dx][0], span[dy][0], pl.ds(6, 2)],
                dst_ref=L0.R.at[span[dx][1], span[dy][1], pl.ds(6, 2)],
                send_sem=send.at[8 + k],
                recv_sem=recv.at[8 + k],
                device_id=(lax.rem(gx + dx + NX, NX), lax.rem(gy + dy + NY, NY)),
                device_id_type=MESH,
            )
        )
    for copy in pending:
        copy.start()
    faces = pending
    sent = []

    def restrict(src, halo_src, count, reach, i):
        row = src[halo_src + 2 * i, pl.ds(halo_src, count)] + src[halo_src + 2 * i + 1, pl.ds(halo_src, count)]
        row = row.reshape(count // 2, 2, 8, 128)
        return pair_sum(row[:, 0] + row[:, 1], reach) * 0.125

    def coarsen_v1(i):
        L1.V[4 + i, pl.ds(4, 8)] = restrict(L0.V, 3, 16, 1, i)

    def coarsen_v2(i):
        L2.V[4 + i, pl.ds(4, 4)] = restrict(L1.V, 4, 8, 2, i)

    loop(0, 8, coarsen_v1)
    loop(0, 4, coarsen_v2)

    def pack_v1(a):
        for b in range(2):
            parts = [by_group([L1.V[4 + 2 * a + p, 4 + 4 * b + k] for k in range(4)]) for p in range(2)]
            VP1[a + 2, b + 1] = jnp.where(lane % 2 == 0, parts[0], parts[1])

    loop(0, 4, pack_v1)
    tile = None
    for p in range(4):
        part = by_group([L2.V[4 + p, 4 + k] for k in range(4)])
        tile = part if tile is None else jnp.where(lane % 4 == p, part, tile)
    VP2[1, 1] = tile

    def inside(lo, hi, margin):
        return [(3 + margin, 19 - margin, 3 + margin, 19 - margin)]

    def around(lo, hi, margin):
        a, b = 3 + margin, 19 - margin
        return [(lo, a, lo, hi), (b, hi, lo, hi), (a, b, lo, a), (a, b, b, hi)]

    for part in inside(1, 21, 1):
        L0.build(gx, gy, kinds, *part)
    L0.descend(inside)
    for copy in pending:
        copy.wait_recv()

    early = halo_copies(VP1, (4, 2), (2, 1), (2, 1), (2, 1), gx, gy, send, recv, 12, 8)
    early += halo_copies(VP2, (1, 1), (1, 1), (1, 1), (1, 1), gx, gy, send, recv, 20, 8)
    for copy in early:
        copy.start()
    sent += early

    for top, bottom, lo, hi in around(0, 22, 0):

        def fill_v0(i):
            for j, m in quad(lo, hi):
                L0.V[i, pl.ds(j, m)] = spread_sub(L0.R[i, pl.ds(j, m)], 3)

        loop(top, bottom, fill_v0, hi - lo)
    for part in around(1, 21, 1):
        L0.build(gx, gy, kinds, *part)
    L0.descend(around)
    for copy in faces:
        copy.wait_send()

    def pack_r1(a):
        one, other = restrict(L0.Q, 3, 16, 1, 2 * a), restrict(L0.Q, 3, 16, 1, 2 * a + 1)
        RP1[a + 1, pl.ds(2, 8)] = choose(lane % 2 == 0, one, other)

    loop(0, 4, pack_r1)
    pending = halo_copies(RP1, (4, 8), (1, 2), (1, 2), (1, 1), gx, gy, send, recv, 28)
    for copy in pending:
        copy.start()
    sent += pending
    for copy in early:
        copy.wait_recv()

    def unpack_v1(a):
        for b in range(4):
            both = VP1[a, b]
            for p in range(2):
                part = pick_lane(both, (lane // 2) * 2 + p)
                for k in range(4):
                    L1.V[2 * a + p, 4 * b + k] = spread_sub(part, k)

    loop(0, 8, unpack_v1)

    def unpack_v2(a):
        for b in range(3):
            both = VP2[a, b]
            for p in range(4):
                part = pick_lane(both, (lane // 4) * 4 + p)
                for k in range(4):
                    L2.V[4 * a + p, 4 * b + k] = spread_sub(part, k)

    loop(0, 3, unpack_v2)
    L1.build(gx, gy, kinds, 1, 15, 1, 15)
    L2.build(gx, gy, kinds, 1, 11, 1, 11)
    for copy in pending:
        copy.wait_recv()

    def unpack_pairs(src, dst, count, x_first, y_first, y_count):
        def body(a):
            row = src[a, pl.ds(0, y_count)]
            for p in range(2):
                dst[x_first + 2 * a + p, pl.ds(y_first, y_count)] = pick_lane(row, (lane // 2) * 2 + p)

        loop(0, count, body)

    unpack_pairs(RP1, L1.R, 6, 2, 2, 12)
    L1.descend()

    def pack_r2(a):
        rows = []
        for p in range(2):
            row = restrict(L1.Q, 4, 8, 2, 2 * a + p).reshape(2, 2, 8, 128)
            rows.append(choose(lane % 2 == 0, row[:, 0], row[:, 1]))
        RP2[a + 1, pl.ds(1, 2)] = choose(lane % 4 < 2, rows[0], rows[1])

    loop(0, 2, pack_r2)
    pending = halo_copies(RP2, (2, 2), (1, 1), (1, 1), (1, 1), gx, gy, send, recv, 36)
    for copy in pending:
        copy.start()
    sent += pending
    late0 = halo_copies(L0.Q, (16, 16), (3, 3), (2, 2), (1, 1), gx, gy, send, recv, 99)
    for copy in late0:
        copy.start()
    sent += late0
    for copy in pending:
        copy.wait_recv()

    def unpack_quads(src, dst, count, first):
        def body(a):
            for b in range(count):
                both = src[a, b]
                for p in range(2):
                    for k in range(2):
                        dst[first + 2 * a + p, first + 2 * b + k] = pick_lane(both, (lane // 4) * 4 + (2 * p + k))

        loop(0, count, body)

    unpack_quads(RP2, L2.R, 4, 2)
    L2.descend()

    for p in range(2):
        r3 = restrict(L2.Q, 4, 4, 4, p)
        v3 = restrict(L2.V, 4, 4, 4, p)
        both = choose(group == 3, v3, r3)
        both = pick_lane(both, 8 * (lane % 16))
        both = jnp.where(tiled(lane // 16 == subs(), both), both, 0.0)
        for k in range(2):
            MSG[pl.ds(2 * p + k, 1), :] = jnp.sum(both[k], axis=0, keepdims=True)
    rows = pl.ds(pl.multiple_of(4 * gy, 4), 4)
    keep = pltpu.make_async_copy(MSG.at[pl.ds(0, 4)], CG.at[pair, core, rows], in_sem.at[0])
    keep.start()
    pending = []
    for k in range(1, 16):
        pending.append(
            pltpu.make_async_remote_copy(
                src_ref=MSG.at[pl.ds(0, 4)],
                dst_ref=CG.at[pair, core, rows],
                send_sem=send.at[44 + k - 1],
                recv_sem=recv.at[44 + k - 1],
                device_id=(lax.rem(gx + 2 * k, NX), gy),
                device_id_type=MESH,
            )
        )
    for copy in pending:
        copy.start()
    sent += pending

    def pack_1(a):
        for src, dst, x0, y0 in ((L1.Q, QP1, 2, 3), (L1.X, XP1, 1, 2)):
            one, other = src[4 + 2 * a, pl.ds(4, 8)], src[5 + 2 * a, pl.ds(4, 8)]
            dst[x0 + a, pl.ds(y0, 8)] = choose(lane % 2 == 0, one, other)

    loop(0, 4, pack_1)

    def pack_2(a):
        for src, dst, x0 in ((L2.Q, QP2, 2), (L2.X, XP2, 1)):
            mixed = []
            for p in range(2):
                row = src[4 + 2 * a + p, pl.ds(4, 4)].reshape(2, 2, 8, 128)
                mixed.append(choose(lane % 2 == 0, row[:, 0], row[:, 1]))
            dst[x0 + a, pl.ds(x0, 2)] = choose(lane % 4 < 2, mixed[0], mixed[1])

    loop(0, 2, pack_2)
    late2 = halo_copies(QP2, (2, 2), (2, 2), (2, 2), (2, 2), gx, gy, send, recv, 67)
    late2 += halo_copies(XP2, (2, 2), (1, 1), (1, 1), (1, 1), gx, gy, send, recv, 75)
    late1 = halo_copies(QP1, (4, 8), (2, 3), (2, 3), (1, 2), gx, gy, send, recv, 83)
    late1 += halo_copies(XP1, (4, 8), (1, 2), (1, 2), (1, 1), gx, gy, send, recv, 91)
    keep.wait()
    for copy in pending:
        copy.wait_recv()

    pending = []
    for k in range(1, 8):
        pending.append(
            pltpu.make_async_remote_copy(
                src_ref=CG.at[:, core, rows],
                dst_ref=CG.at[:, core, rows],
                send_sem=send.at[59 + k - 1],
                recv_sem=recv.at[59 + k - 1],
                device_id=(gx, lax.rem(gy + k, NY)),
                device_id_type=MESH,
            )
        )
    for copy in pending:
        copy.start()
    sent += pending
    for copy in pending:
        copy.wait_recv()
    swap = pltpu.make_async_remote_copy(
        src_ref=CG.at[:, core],
        dst_ref=CG.at[:, core],
        send_sem=send.at[66],
        recv_sem=recv.at[66],
        device_id=(gx + 1 - 2 * core, gy),
        device_id_type=MESH,
    )
    swap.start()
    sent.append(swap)
    for copy in late2 + late1:
        copy.start()
    sent += late2 + late1
    swap.wait_recv()

    coarse(gx, gy, kinds, CG, CR, CV, KXM, KXP, KA, KB, KZ, CD, CI, CSA, CSB, CRB, CE)

    flat = CE.reshape(96, 128)

    def expand(a):
        for j in range(6):
            row = 16 * a + 8 * (j % 2) + lax.rem(gy + 7 + j // 2, 8)
            both = jnp.broadcast_to(flat[pl.ds(row, 1), :], (8, 128))
            both = pick_lane(both, 16 * subs() + lane // 8)
            for p in range(2):
                for k in range(2):
                    L2.PR[2 * a + p, 2 * j + k] = both

    loop(0, 6, expand)

    for copy in late2:
        copy.wait_recv()
    unpack_quads(QP2, L2.Q, 6, 0)
    unpack_quads(XP2, L2.X, 4, 2)

    def middle(level):
        h, b = level.halo, level.block
        level.correct(h - 3, h + b + 3)
        level.second_step(level.R, level.R, h - 2, h + b + 2, h - 2, h + b + 2)

        def body(i):
            for j, m in quad(h - 2, h + b + 2):
                here = pl.ds(j, m)
                level.SB[i, here] = (level.X[i, here] + level.PR[i, here]) + (level.SA[i, here] + level.SB[i, here])

        loop(h - 2, h + b + 2, body)

    middle(L2)
    L1.lift(L2.SB, (0, 2), 2, 8)
    for copy in late1:
        copy.wait_recv()

    def unpack_q1(a):
        row = QP1[a]
        for p in range(2):
            L1.Q[2 * a + p, pl.ds(1, 14)] = pick_lane(row, (lane // 2) * 2 + p)

    loop(0, 8, unpack_q1)
    unpack_pairs(XP1, L1.X, 6, 2, 2, 12)
    middle(L1)
    L0.lift(L1.SB, (1, 2), 2, 12)
    for copy in late0:
        copy.wait_recv()
    L0.correct(1, 21)
    L0.second_step(L0.R, L0.R, 2, 20, 2, 20)

    def last(i):
        for j, m in quad(3, 19):
            here = pl.ds(j, m)
            step, near = L0.near(L0.SB, i, j, m)
            diag = L0.D[i, here]
            field = (L0.X[i, here] + L0.PR[i, here]) + (L0.SA[i, here] + step)
            L0.R[i, here] = L0.R[i, here] - diag * step + near
            OW[i - 3, pl.ds(j - 3, m)] = diag * field

    stores = []
    for half in range(2):
        loop(3 + 8 * half, 11 + 8 * half, last)
        rows = pl.ds(8 * half, 8)
        for c in range(3):
            for s in range(2):
                spot = pl.ds(128 * s, 128)
                for src, dst in (
                    (OW.at[rows, :, 2 * c + s], out_w),
                    (L0.R.at[pl.ds(3 + 8 * half, 8), pl.ds(3, 16), 2 * c + s], out_r),
                ):
                    copy = pltpu.make_async_copy(src, dst.at[c, rows, :, spot], in_sem.at[len(stores)])
                    copy.start()
                    stores.append(copy)
    for copy in sent:
        copy.wait_send()
    for copy in stores:
        copy.wait()


def coarse(gx, gy, kinds, CG, CR, CV, KXM, KXP, KA, KB, KZ, CD, CI, CSA, CSB, CRB, CE):
    planes = 2 * NX
    scale = 0.25 ** (LEVELS - 1)
    lane = lanes()
    spot = lane % 32
    flat = CG.reshape(1024, 128)

    def blocks(reach, body):
        lo = jnp.maximum(2 * gx - 2 - reach, 0) // BLOCK
        hi = (jnp.minimum(2 * gx + 4 + reach, planes) + BLOCK - 1) // BLOCK
        loop(lo, hi, body)

    zeros = jnp.zeros((PAD, 2, 8, 128), F32)
    for place in (0, PAD + planes):
        CV[pl.ds(place, PAD)] = zeros
        CSA[pl.ds(place, PAD)] = zeros
        CSB[pl.ds(place, PAD)] = zeros

    def take(b):
        for q in range(BLOCK):
            for y in range(2):
                start = 16 * BLOCK * b + 32 * (q // 2) + 2 * (q % 2) + y
                row = flat[pl.ds(start, 8, stride=4), :]
                CR[PAD + BLOCK * b + q, y] = row
                CV[PAD + BLOCK * b + q, y] = pick_lane(row, 96 + spot)

    blocks(26, take)

    def per_kind(wall):
        tile = jnp.zeros((8, 128), F32)
        for c in range(3):
            tile = jnp.where(lane // 32 == c, kinds[c, wall].astype(F32), tile)
        return tile

    walls = [per_kind(wall) for wall in range(6)]
    z_wall = jnp.where(spot == 0, walls[4], 0.0) + jnp.where(spot == 31, walls[5], 0.0)
    low_y = z_wall + jnp.where(subs() == 0, walls[2], 0.0)
    high_y = z_wall + jnp.where(subs() == 7, walls[3], 0.0)

    def setup(b):
        here = pl.ds(PAD + BLOCK * b, BLOCK)
        prev, after = pl.ds(PAD - 1 + BLOCK * b, BLOCK), pl.ds(PAD + 1 + BLOCK * b, BLOCK)
        plane = lax.broadcasted_iota(jnp.int32, (BLOCK, 8, 128), 0) + BLOCK * b
        even, odd = CV[here, 0], CV[here, 1]
        half = 0.5 * scale
        ka = half * (even + odd)
        kb = half * (odd + roll_sub(even, -1))
        kb = jnp.where(tiled(subs() == 7, kb), 0.0, kb)
        KA[here] = ka
        KB[here] = kb
        x_wall = jnp.where(plane == 0, tiled(walls[0], even), 0.0)
        x_wall = x_wall + jnp.where(plane == planes - 1, tiled(walls[1], even), 0.0)
        for y, value, wall, other in ((0, even, low_y, roll_sub(kb, 1)), (1, odd, high_y, kb)):
            kxm = jnp.where(plane == 0, 0.0, half * (CV[prev, y] + value))
            kxp = jnp.where(plane == planes - 1, 0.0, half * (value + CV[after, y]))
            kz = half * (value + roll_lane(value, -1))
            kz = jnp.where(tiled(spot == 31, kz), 0.0, kz)
            KXM[here, y] = kxm
            KXP[here, y] = kxp
            KZ[here, y] = kz
            total = (kxm + kxp) + (ka + other) + (kz + roll_lane(kz, 1))
            total = total + (2.0 * scale) * value * (x_wall + tiled(wall, value))
            CD[here, y] = total
            inverse = 1.0 / total
            CI[here, y] = inverse
            CSA[here, y] = CR[here, y] * inverse * (1.0 / CMID)

    blocks(25, setup)

    own = pl.ds(PAD - 2 + 2 * gx, 6)
    CE[...] = CSA[own]

    def sweep(rho, reach, now, later, r_now, r_later):
        rho_next = 1.0 / (2.0 * CSIG - rho)
        step_a = rho_next * rho
        step_b = rho_next * (2.0 / CRAD)
        size = 6 + 2 * reach
        start = PAD + jnp.minimum(jnp.maximum(2 * gx - 2 - reach, 0), planes - size)
        for first in range(0, size, PLANES):
            count = min(PLANES, size - first)
            here = pl.ds(start + first, count)
            prev, after = pl.ds(start + first - 1, count), pl.ds(start + first + 1, count)
            even, odd = now[here, 0], now[here, 1]
            ka, kb = KA[here], KB[here]
            for y, value, beside in (
                (0, even, ka * odd + roll_sub(kb * odd, 1)),
                (1, odd, ka * even + kb * roll_sub(even, -1)),
            ):
                kz = KZ[here, y]
                near = KXM[here, y] * now[prev, y] + KXP[here, y] * now[after, y] + beside
                near = near + (kz * roll_lane(value, -1) + roll_lane(kz * value, 1))
                r = r_now[here, y] - CD[here, y] * value + near
                r_later[here, y] = r
                later[here, y] = tiled(step_a, r) * value + tiled(step_b, r) * (r * CI[here, y])
        CE[...] = CE[...] + later[own]
        return rho_next

    def two(reach):
        def body(_, rho):
            rho = sweep(rho, reach, CSA, CSB, CR, CRB)
            return sweep(rho, reach, CSB, CSA, CRB, CR)

        return body

    rho = jnp.full((8, 128), 1.0 / CSIG, F32)
    for first in range(0, CSWEEPS - 1, 4):
        reach = CSWEEPS - 2 - first
        pairs = min(4, CSWEEPS - 1 - first) // 2
        rho = lax.fori_loop(0, pairs, two(reach), rho)
    if (CSWEEPS - 1) % 2:
        sweep(rho, 0, CSA, CSB, CR, CRB)


def per_device(body_force, phase, viscosity_table, wall_kinds):
    def vmem(*lead):
        return pltpu.VMEM(lead + (8, 128), F32)

    scratch = [
        pltpu.VMEM((16, 16, 8, 128), jnp.int32),
        vmem(6, 12), vmem(8, 4), vmem(8, 14), vmem(6, 12),
        vmem(4, 4), vmem(3, 3), vmem(6, 6), vmem(4, 4),
        vmem(), pltpu.VMEM((16, 2, 32, 128), F32),
    ]
    depth = 2 * NX + 2 * PAD
    scratch += [vmem(depth, 2)] * 4 + [vmem(depth)] * 2 + [vmem(depth, 2)] * 3 + [vmem(depth, 2)] * 3 + [vmem(6, 2)]
    scratch += [vmem(16, 16)]
    for frame in (22, 16, 12):
        scratch += [vmem(frame, frame)] * 12
    n_sems = 107
    scratch += [pltpu.SemaphoreType.DMA((24,)), pltpu.SemaphoreType.DMA((n_sems,)), pltpu.SemaphoreType.DMA((n_sems,))]
    shape = jax.ShapeDtypeStruct(body_force.shape, F32)
    return pl.pallas_call(
        kernel,
        out_shape=(shape, shape),
        in_specs=[
            pl.BlockSpec(memory_space=pl.ANY),
            pl.BlockSpec(memory_space=pl.ANY),
            pl.BlockSpec(memory_space=pltpu.SMEM),
            pl.BlockSpec(memory_space=pltpu.SMEM),
        ],
        out_specs=(pl.BlockSpec(memory_space=pl.ANY), pl.BlockSpec(memory_space=pl.ANY)),
        scratch_shapes=scratch,
        compiler_params=pltpu.CompilerParams(
            collective_id=0, has_side_effects=True, vmem_limit_bytes=56 * 2**20
        ),
        name="vcycle",
    )(body_force, phase, viscosity_table, wall_kinds)


def solution(mesh):
    placed = (P(None, "gx", "gy", None), P("gx", "gy", None), P(), P())
    return jax.shard_map(
        per_device,
        mesh=mesh,
        in_specs=placed,
        out_specs=(P(None, "gx", "gy", None), P(None, "gx", "gy", None)),
        check_vma=False,
    )
```
